32 devices in a mesh: row: 4 (over x, core), real: 8 (over z, y).
Axes of the slice: x: 2, y: 2, z: 4, core: 2. Of those that a mesh axis runs over, the one named last changes fastest.
Arguments:
- right_sides: float32 [10, 4, 256, 4096], P(None, 'row', None, 'real'), may hold values from -8 to 8
- factor: float32 [10, 4, 256, 1024], P(None, 'row', None, 'real'), may hold values from -1 to 2, as said below
Outputs:
- updated: float32 [10, 4, 256, 4096], P(None, 'row', None, 'real')
The draws below stay inside these ranges and needn't reach their ends.
Inputs may be any that keep to these rules, and one draw needn't show every extreme that they name: factor is lower triangular in global row and column order (entries with column above the global row are 0), with diagonal entries from 1 to 2.
All inputs are finite; a program needn't handle non-finite values.
Results may differ from the reference program's by a relative error of at most 0.0001.
Values sent between devices are 32-bit elements; how exact they have to be, the bound alone decides.
No kernel may reach another device: no remote copies, remote signals or barrier semaphores. Data moves between devices by JAX's collectives and lax.ppermute only.
A program may use at most 128 MiB of HBM per device.

```python
import math
import jax
import jax.numpy as jnp
from jax import lax

PANEL = 256
BLK_DEV = 10
WINDOW = 1024
ACTIVE = 10240
NRHS = 4096
N_ROW = 4


def draw_factor(key, part):
    first_key, second_key = jax.random.split(key, 2)
    full_shape = (BLK_DEV, N_ROW, PANEL, WINDOW)
    coupling = jax.random.normal(first_key, full_shape, jnp.float32)
    coupling = coupling / math.sqrt(WINDOW)
    diagonal_vals = jax.random.uniform(second_key, (BLK_DEV, N_ROW, PANEL, 1), jnp.float32, 1.0, 2.0)
    block_index = jnp.arange(BLK_DEV)[:, None] * N_ROW + jnp.arange(N_ROW)[None, :]
    row_index = block_index[:, :, None, None] * PANEL + jnp.arange(PANEL)[None, None, :, None]
    col_index = jnp.arange(WINDOW)[None, None, None, :]
    below_mask = col_index < row_index
    on_diagonal = col_index == row_index
    return jnp.where(below_mask, coupling, 0.0) + jnp.where(on_diagonal, diagonal_vals, 0.0)


def levels(own_key, extent, cuts, least, largest):
    factor_of = 1.0
    for position, blocks in cuts:
        heights = jax.random.uniform(jax.random.fold_in(jax.random.fold_in(own_key, 6), position), (blocks,), jnp.float32, least / len(cuts), largest / len(cuts))
        factor_of = factor_of * jnp.repeat(jnp.exp(heights), extent[position] // blocks).reshape((-1,) + (1,) * (len(extent) - 1 - position))
    return factor_of


def noise(own_key, dims, deviation, reach, cuts=(), dtype=jnp.bfloat16):
    gain = levels(own_key, dims, cuts, -0.22, 0.18) if cuts else 1.0
    array = jax.random.normal(own_key, dims, jnp.float32) * deviation * gain
    return jnp.minimum(jnp.maximum(array, -reach), reach).astype(dtype)


def setup_inputs(seed: int = 0) -> dict:
    streams_of = jax.random.split(jax.random.key(seed), 3)
    return {
        "right_sides": noise(streams_of[0], (BLK_DEV, N_ROW, PANEL, NRHS), 1.0, 8.0, ((1, 4), (3, 8)), jnp.float32),
        "factor": draw_factor(jax.random.fold_in(streams_of[2], 71), 0),
    }


def reference(right_sides, factor):
    working = right_sides.reshape(ACTIVE, NRHS)
    matrix = factor.reshape(ACTIVE, WINDOW)
    for panel_index in range(N_ROW):
        lower_edge = panel_index * PANEL
        upper_edge = lower_edge + PANEL
        diagonal_block = matrix[lower_edge:upper_edge, lower_edge:upper_edge]
        answer = lax.linalg.triangular_solve(diagonal_block, working[lower_edge:upper_edge], left_side=True, lower=True)
        below = working[upper_edge:] - jnp.dot(matrix[upper_edge:, lower_edge:upper_edge], answer, precision=lax.Precision.HIGHEST)
        working = jnp.concatenate([working[:lower_edge], answer, below], axis=0)
    return working.reshape(BLK_DEV, N_ROW, PANEL, NRHS)
```

```python
import functools

import jax
import jax.numpy as jnp
from jax import lax
from jax.experimental import pallas as pl
from jax.experimental.pallas import tpu as pltpu
from jax.sharding import PartitionSpec as P

F32, BF16 = jnp.float32, jnp.bfloat16
TILE, HALF, BASE = 128, 64, 16


def split(value):
    high = value.astype(BF16)
    return high, (value - high.astype(F32)).astype(BF16)


def product(a_high, a_low, b_high, b_low):
    dot = functools.partial(jnp.dot, preferred_element_type=F32)
    return dot(a_high, b_high) + (dot(a_high, b_low) + dot(a_low, b_high))


def exact(a, b):
    return jnp.dot(a, b, precision=lax.Precision.HIGHEST, preferred_element_type=F32)


def half_inverses(tiles):
    count = len(tiles)
    lane = lax.broadcasted_iota(jnp.int32, (BASE, TILE), 1)
    row = lax.broadcasted_iota(jnp.int32, (BASE, TILE), 0)
    packed = []
    for tile in tiles:
        kept = jnp.zeros((BASE, TILE), F32)
        for g in range(TILE // BASE):
            kept = jnp.where(lane // BASE == g, tile[g * BASE : (g + 1) * BASE], kept)
        packed.append(kept)
    packed = jnp.concatenate(packed, axis=0)
    k = lax.broadcasted_iota(jnp.int32, (TILE, TILE), 0)
    m = lax.broadcasted_iota(jnp.int32, (TILE, TILE), 1)
    x = jnp.broadcast_to((row == lane % BASE).astype(F32)[None], (count, BASE, TILE))
    for j in range(BASE):
        spread = (k == (m // BASE) * BASE + j).astype(F32)
        column = exact(packed, spread).reshape(count, BASE, TILE)
        solved = x[:, j : j + 1] / column[:, j : j + 1]
        x = jnp.where(row[None] == j, solved, x - column * solved)
    inverses = []
    for t, tile in enumerate(tiles):
        w = jnp.where(k // BASE == m // BASE, jnp.concatenate([x[t]] * (TILE // BASE), axis=0), 0.0)
        size = BASE
        while size < HALF:
            joined = (k // (2 * size) == m // (2 * size)) & (k // size != m // size)
            w = w - exact(exact(w, jnp.where(joined, tile, 0.0)), w)
            size *= 2
        inverses.append(w)
    return inverses


def solve_kernel(codes, place, head_refs, side_refs, y_ref, l_high, l_low, y_high, y_low):
    rows = head_refs[0].shape[-2]
    window = l_high.shape[0]
    position = place[0]
    diagonals = pl.ds(0, 1)
    for code, head, side in zip(codes, head_refs, side_refs):
        at = pl.ds(pl.multiple_of((position ^ code) * rows, rows), rows)
        high, low = split(head[...])
        l_high[at] = high
        l_low[at] = low
        y_ref[at] = side[...]
    tiles = []
    for t in range(window // TILE):
        at = slice(t * TILE, (t + 1) * TILE)
        tiles.append(l_high[at, at].astype(F32) + l_low[at, at].astype(F32))
    inverses = half_inverses(tiles)
    for t in range(window // TILE):
        begin = t * TILE
        value = y_ref[begin : begin + TILE]
        if t:
            value = value - product(
                l_high[begin : begin + TILE, :begin],
                l_low[begin : begin + TILE, :begin],
                y_high[:begin],
                y_low[:begin],
            )
        w = inverses[t]
        for h in range(TILE // HALF):
            part = value[h * HALF : (h + 1) * HALF]
            at = slice(begin + h * HALF, begin + (h + 1) * HALF)
            if h:
                inside = slice(begin, begin + h * HALF)
                part = part - product(
                    l_high[at, inside], l_low[at, inside], y_high[inside], y_low[inside]
                )
            inv = w[h * HALF : (h + 1) * HALF, h * HALF : (h + 1) * HALF]
            answer = product(*split(inv), *split(part))
            y_ref[at] = answer
            high, low = split(answer)
            y_high[at] = high
            y_low[at] = low


def solve(position, codes, heads, sides):
    window = heads[0].shape[-1]
    columns = sides[0].shape[-1]
    count = len(codes)

    def kernel(place, *refs):
        solve_kernel(codes, place, refs[:count], refs[count : 2 * count], *refs[2 * count :])

    whole = pl.BlockSpec(memory_space=pltpu.VMEM)
    return pl.pallas_call(
        kernel,
        out_shape=jax.ShapeDtypeStruct((window, columns), F32),
        in_specs=[pl.BlockSpec(memory_space=pltpu.SMEM)] + [whole] * (2 * count),
        out_specs=whole,
        scratch_shapes=[
            pltpu.VMEM((window, window), BF16),
            pltpu.VMEM((window, window), BF16),
            pltpu.VMEM((window, columns), BF16),
            pltpu.VMEM((window, columns), BF16),
        ],
        compiler_params=pltpu.CompilerParams(vmem_limit_bytes=40 << 20),
        cost_estimate=pl.CostEstimate(
            flops=6 * window * window * columns, bytes_accessed=4 * window * (window + 2 * columns), transcendentals=0
        ),
        name="solve",
    )(position, *heads, *sides)


def update(y, places, pieces, base, first, target=None, solved=None):
    blocks, rows, _ = pieces[0].shape
    columns = y.shape[1]
    widths = [piece.shape[-1] for piece in pieces]
    count = len(pieces)
    depth = sum(widths)
    in_place = target is base

    def kernel(place, *refs):
        y_ref, base_ref = refs[0], refs[1]
        piece_refs = refs[2 : 2 + count]
        out_ref, y_high, y_low = refs[-3:]

        @pl.when(pl.program_id(0) == 0)
        def _():
            begin = 0
            for n, width in enumerate(widths):
                high, low = split(y_ref[pl.ds(pl.multiple_of(place[n] * width, width), width)])
                y_high[begin : begin + width] = high
                y_low[begin : begin + width] = low
                begin += width

        wide = jnp.concatenate([ref[0] for ref in piece_refs], axis=1)
        out_ref[0, 0] = base_ref[0, 0] - product(*split(wide), y_high[...], y_low[...])

    block = pl.BlockSpec((1, 1, rows, columns), lambda i, *_: (i + first, 0, 0, 0))
    specs = [pl.BlockSpec((y.shape[0], columns), lambda i, *_: (0, 0)), block]
    specs += [pl.BlockSpec((1, rows, width), lambda i, *_: (i, 0, 0)) for width in widths]
    operands = [y, base, *pieces]
    aliases = {}
    if in_place:
        aliases = {2: 0}
    elif target is not None:
        specs.append(pl.BlockSpec(memory_space=pl.ANY))
        operands.append(target)
        aliases = {len(operands): 0}
    return pl.pallas_call(
        kernel,
        out_shape=jax.ShapeDtypeStruct(base.shape, F32),
        grid_spec=pltpu.PrefetchScalarGridSpec(
            num_scalar_prefetch=1,
            grid=(blocks,),
            in_specs=specs,
            out_specs=block,
            scratch_shapes=[pltpu.VMEM((depth, columns), BF16), pltpu.VMEM((depth, columns), BF16)],
        ),
        input_output_aliases=aliases,
        compiler_params=pltpu.CompilerParams(vmem_limit_bytes=40 << 20),
        cost_estimate=pl.CostEstimate(
            flops=6 * blocks * rows * depth * columns,
            bytes_accessed=4 * blocks * rows * (depth + 2 * columns),
            transcendentals=0,
        ),
        name="update",
    )(places, *operands)


def place_head(y, position, target):
    _, _, rows, columns = target.shape

    def kernel(place, y_ref, target_ref, out_ref):
        out_ref[0, 0] = y_ref[...]

    return pl.pallas_call(
        kernel,
        out_shape=jax.ShapeDtypeStruct(target.shape, F32),
        grid_spec=pltpu.PrefetchScalarGridSpec(
            num_scalar_prefetch=1,
            grid=(1,),
            in_specs=[
                pl.BlockSpec((rows, columns), lambda i, place: (place[0], 0)),
                pl.BlockSpec(memory_space=pl.ANY),
            ],
            out_specs=pl.BlockSpec((1, 1, rows, columns), lambda i, place: (0, 0, 0, 0)),
        ),
        input_output_aliases={2: 0},
        name="place_head",
    )(position, y, target)


def over_row(block, size):
    codes, held = [0], [block]
    bit = size // 2
    while bit:
        pairs = [(n, n ^ bit) for n in range(size)]
        held = held + [lax.ppermute(value, "row", pairs) for value in held]
        codes = codes + [code ^ bit for code in codes]
        bit //= 2
    return codes, held


def ring_of_pairs():
    lanes = 2
    at = lambda z, lane: z * lanes + lane
    each = lambda pairs: [(at(a, lane), at(b, lane)) for a, b in pairs for lane in range(lanes)]
    across = lambda zs: [(at(z, lane), at(z, 1 - lane)) for z in zs for lane in range(lanes)]
    return {
        "ends": each([(0, 1), (1, 0), (2, 3), (3, 2)]),
        "out": each([(1, 0), (2, 3)]),
        "middle": each([(1, 2), (2, 1)]),
        "across": across(range(4)),
        "across_outer": across((0, 3)),
    }


def body(right_sides, factor):
    row_count, real_count = lax.axis_size("row"), lax.axis_size("real")
    position = lax.axis_index("row")[None]
    mine = factor[:, 0]
    head = lax.all_gather(mine[0], "real", axis=1, tiled=True)
    codes, sides = over_row(right_sides[0, 0], row_count)
    codes, heads = over_row(head, row_count)
    y = solve(position, codes, heads, sides)
    if real_count != 8:
        rest = lax.all_gather(mine[1:], "real", axis=2, tiled=True)
        out = update(y, jnp.zeros((1,), jnp.int32), [rest], right_sides, 1)
        return place_head(y, position, out)

    ways = ring_of_pairs()
    move = lambda value, way: lax.ppermute(value, "real", ways[way])
    here = lax.axis_index("real")
    z, lane = here // 2, here % 2
    outer = (z == 0) | (z == 3)
    pick = lambda a, b: jnp.where(outer, a, b)
    trailing = mine.shape[0] - 1
    cut = 1 + (trailing + 1) // 2
    own = [mine[1:cut], mine[cut:]]
    ends, mid, side, ends2, mid2, side2, ends3, side3 = ([None, None] for _ in range(8))
    for k in range(2):
        ends[k] = move(own[k], "ends")
        mid[k] = move(own[k], "middle")
        side[k] = move(own[k], "across")
    for k in range(2):
        ends2[k] = move(pick(side[k], mid[k]), "ends")
        mid2[k] = move(ends[k], "middle")
        side2[k] = move(pick(ends[k], mid[k]), "across")
    for k in (1, 0):
        side3[k] = move(pick(ends2[k], mid2[k]), "across")
    for k in range(2):
        ends3[k] = move(mid2[k], "out")
    last = [move(ends3[0], "across_outer"), move(side3[1], "out")]

    mirror = 3 - z
    partner = jnp.where(z < 2, 1 - z, 5 - z)
    other = 3 - partner
    spot = lambda at, which: at * 2 + which
    places = jnp.stack(
        [
            here,
            spot(partner, lane),
            spot(z, 1 - lane),
            jnp.where(outer, spot(other, lane), spot(partner, 1 - lane)),
            jnp.where(outer, spot(partner, 1 - lane), spot(mirror, 1 - lane)),
            jnp.where(outer, here, spot(mirror, lane)),
            jnp.where(outer, spot(mirror, lane), here),
            jnp.where(outer, here, spot(other, lane)),
            jnp.where(outer, spot(other, 1 - lane), spot(other, 1 - lane)),
        ]
    ).astype(jnp.int32)
    out = None
    for k, first in ((0, 1), (1, cut)):
        pieces = [own[k], ends[k], side[k], ends2[k], side2[k], mid[k], ends3[k], mid2[k], side3[k]]
        out = update(y, places, pieces, right_sides, first, target=out)
    out = place_head(y, position, out)
    final = jnp.where(outer, spot(mirror, 1 - lane), here)[None].astype(jnp.int32)
    for k, first in ((1, cut), (0, 1)):
        out = update(y, final, [last[k]], out, first, target=out)
    return out


def solution(mesh):
    placed = (P(None, "row", None, "real"), P(None, "row", None, "real"))
    return jax.shard_map(
        body, mesh=mesh, in_specs=placed, out_specs=P(None, "row", None, "real"), check_vma=False
    )
```

```python
import functools

import jax
import jax.numpy as jnp
from jax import lax
from jax.experimental import pallas as pl
from jax.experimental.pallas import tpu as pltpu
from jax.sharding import PartitionSpec as P

F32, BF16 = jnp.float32, jnp.bfloat16
TILE, HALF, BASE = 128, 64, 16


def split(value):
    high = value.astype(BF16)
    return high, (value - high.astype(F32)).astype(BF16)


def product(a_high, a_low, b_high, b_low):
    dot = functools.partial(jnp.dot, preferred_element_type=F32)
    return dot(a_high, b_high) + (dot(a_high, b_low) + dot(a_low, b_high))


def exact(a, b):
    return jnp.dot(a, b, precision=lax.Precision.HIGHEST, preferred_element_type=F32)


def half_inverses(tiles):
    count = len(tiles)
    lane = lax.broadcasted_iota(jnp.int32, (BASE, TILE), 1)
    row = lax.broadcasted_iota(jnp.int32, (BASE, TILE), 0)
    packed = []
    for tile in tiles:
        kept = jnp.zeros((BASE, TILE), F32)
        for g in range(TILE // BASE):
            kept = jnp.where(lane // BASE == g, tile[g * BASE : (g + 1) * BASE], kept)
        packed.append(kept)
    packed = jnp.concatenate(packed, axis=0)
    k = lax.broadcasted_iota(jnp.int32, (TILE, TILE), 0)
    m = lax.broadcasted_iota(jnp.int32, (TILE, TILE), 1)
    x = jnp.broadcast_to((row == lane % BASE).astype(F32)[None], (count, BASE, TILE))
    for j in range(BASE):
        spread = (k == (m // BASE) * BASE + j).astype(F32)
        column = exact(packed, spread).reshape(count, BASE, TILE)
        solved = x[:, j : j + 1] / column[:, j : j + 1]
        x = jnp.where(row[None] == j, solved, x - column * solved)
    inverses = []
    for t, tile in enumerate(tiles):
        w = jnp.where(k // BASE == m // BASE, jnp.concatenate([x[t]] * (TILE // BASE), axis=0), 0.0)
        size = BASE
        while size < HALF:
            joined = (k // (2 * size) == m // (2 * size)) & (k // size != m // size)
            w = w - exact(exact(w, jnp.where(joined, tile, 0.0)), w)
            size *= 2
        inverses.append(w)
    return inverses


def solve_kernel(codes, counts, place, head_refs, side_refs, y_ref, l_high, l_low, y_high, y_low, landing, head_sems, side_sems):
    rows, width = head_refs[0].shape[-2:]
    window = l_high.shape[0]
    per_row = len(head_refs) // len(codes)
    head_copies, side_copies = [], []
    for c, code in enumerate(codes):
        at = pl.ds(pl.multiple_of((place[0] ^ code) * rows, rows), rows)
        begin = c * sum(counts)
        for p in range(per_row):
            n = c * per_row + p
            into = landing.at[begin : begin + counts[p]]
            head_copies.append(pltpu.make_async_copy(head_refs[n], into, head_sems.at[n]))
            begin += counts[p]
        side_copies.append(pltpu.make_async_copy(side_refs[c], y_ref.at[at], side_sems.at[c]))
    for copy in head_copies + side_copies:
        copy.start()
    for c, code in enumerate(codes):
        at = pl.ds(pl.multiple_of((place[0] ^ code) * rows, rows), rows)
        n = c * sum(counts)
        for p in range(per_row):
            head_copies[c * per_row + p].wait()
            for k in range(counts[p]):
                across = pl.ds(pl.multiple_of(place[1 + n] * width, width), width)
                high, low = split(landing[n])
                l_high[at, across] = high
                l_low[at, across] = low
                n += 1
    for copy in side_copies:
        copy.wait()
    tiles = []
    for t in range(window // TILE):
        at = slice(t * TILE, (t + 1) * TILE)
        tiles.append(l_high[at, at].astype(F32) + l_low[at, at].astype(F32))
    inverses = half_inverses(tiles)
    for t in range(window // TILE):
        begin = t * TILE
        value = y_ref[begin : begin + TILE]
        if t:
            value = value - product(
                l_high[begin : begin + TILE, :begin],
                l_low[begin : begin + TILE, :begin],
                y_high[:begin],
                y_low[:begin],
            )
        w = inverses[t]
        for h in range(TILE // HALF):
            part = value[h * HALF : (h + 1) * HALF]
            at = slice(begin + h * HALF, begin + (h + 1) * HALF)
            if h:
                inside = slice(begin, begin + h * HALF)
                part = part - product(
                    l_high[at, inside], l_low[at, inside], y_high[inside], y_low[inside]
                )
            inv = w[h * HALF : (h + 1) * HALF, h * HALF : (h + 1) * HALF]
            answer = product(*split(inv), *split(part))
            y_ref[at] = answer
            high, low = split(answer)
            y_high[at] = high
            y_low[at] = low


def solve(position, codes, heads, owners, sides):
    counts = [part.shape[0] for part in heads[0]]
    window = sum(counts) * heads[0][0].shape[-1]
    columns = sides[0].shape[-1]
    flat = [part for parts in heads for part in parts]
    total = len(flat)
    place = jnp.concatenate([position] + [owners] * len(codes))

    def kernel(place, *refs):
        head_refs, side_refs = refs[:total], refs[total : total + len(codes)]
        solve_kernel(codes, counts, place, head_refs, side_refs, *refs[total + len(codes) :])

    return pl.pallas_call(
        kernel,
        out_shape=jax.ShapeDtypeStruct((window, columns), F32),
        in_specs=[pl.BlockSpec(memory_space=pltpu.SMEM)] + [pl.BlockSpec(memory_space=pl.ANY)] * (total + len(codes)),
        out_specs=pl.BlockSpec(memory_space=pltpu.VMEM),
        scratch_shapes=[
            pltpu.VMEM((window, window), BF16),
            pltpu.VMEM((window, window), BF16),
            pltpu.VMEM((window, columns), BF16),
            pltpu.VMEM((window, columns), BF16),
            pltpu.VMEM((len(codes) * sum(counts), *flat[0].shape[1:]), F32),
            pltpu.SemaphoreType.DMA((total,)),
            pltpu.SemaphoreType.DMA((len(codes),)),
        ],
        compiler_params=pltpu.CompilerParams(vmem_limit_bytes=48 << 20),
        cost_estimate=pl.CostEstimate(
            flops=30 * window * window * columns, bytes_accessed=4 * window * (window + 2 * columns), transcendentals=0
        ),
        name="solve",
    )(place, *flat, *sides)


def update(y, position, places, pieces, base, first, target=None, with_head=False):
    flat = [part for piece in pieces for part in piece]
    blocks, rows, _ = flat[0].shape
    columns = y.shape[1]
    widths = [piece[0].shape[-1] for piece in pieces]
    count = len(flat)
    depth = sum(widths)
    skip = int(with_head)

    def kernel(place, *refs):
        y_ref, base_ref = refs[0], refs[1]
        piece_refs = list(refs[2 : 2 + count])
        out_ref, y_high, y_low = refs[-3:]

        @pl.when(pl.program_id(0) == 0)
        def _():
            begin = 0
            for n, width in enumerate(widths):
                high, low = split(y_ref[pl.ds(pl.multiple_of(place[n + 1] * width, width), width)])
                y_high[begin : begin + width] = high
                y_low[begin : begin + width] = low
                begin += width

        def below():
            columns_of = iter(piece_refs)
            wide = [sum(next(columns_of)[0] for _ in piece) for piece in pieces]
            high, low = split(jnp.concatenate(wide, axis=1))
            out_ref[0, 0] = base_ref[0, 0] - product(high, low, y_high[...], y_low[...])

        if skip:

            @pl.when(pl.program_id(0) == 0)
            def _():
                out_ref[0, 0] = y_ref[pl.ds(pl.multiple_of(place[0] * rows, rows), rows)]

            pl.when(pl.program_id(0) > 0)(below)
        else:
            below()

    block = pl.BlockSpec((1, 1, rows, columns), lambda i, *_: (i + first - skip, 0, 0, 0))
    specs = [pl.BlockSpec((y.shape[0], columns), lambda i, *_: (0, 0)), block]
    specs += [pl.BlockSpec((1, rows, part.shape[-1]), lambda i, *_: (jnp.maximum(i - skip, 0), 0, 0)) for part in flat]
    operands = [y, base, *flat]
    aliases = {}
    if target is not None:
        specs.append(pl.BlockSpec(memory_space=pl.ANY))
        operands.append(target)
        aliases = {len(operands): 0}
    return pl.pallas_call(
        kernel,
        out_shape=jax.ShapeDtypeStruct(base.shape, F32),
        grid_spec=pltpu.PrefetchScalarGridSpec(
            num_scalar_prefetch=1,
            grid=(blocks + skip,),
            in_specs=specs,
            out_specs=block,
            scratch_shapes=[pltpu.VMEM((depth, columns), BF16), pltpu.VMEM((depth, columns), BF16)],
        ),
        input_output_aliases=aliases,
        compiler_params=pltpu.CompilerParams(vmem_limit_bytes=48 << 20),
        cost_estimate=pl.CostEstimate(
            flops=6 * blocks * rows * depth * columns,
            bytes_accessed=4 * blocks * rows * (depth + 2 * columns),
            transcendentals=0,
        ),
        name="update",
    )(jnp.concatenate([position, places]), *operands)


def finish(y, place, piece, out, first):
    offsets = [offset for _, offset in piece]
    piece = [part for part, _ in piece]
    blocks = min(part.shape[0] for part in piece)
    _, rows, width = piece[0].shape
    columns = y.shape[1]
    count = len(piece)

    def kernel(place, y_ref, *refs):
        y_high, y_low = split(y_ref[...])
        high, low = split(sum(ref[0] for ref in refs[:count]))
        wide = jnp.concatenate([high, low, high], axis=1)
        stack = jnp.concatenate([y_high, y_high, y_low], axis=0)
        refs[-1][0, 0] = refs[count][0, 0] - jnp.dot(wide, stack, preferred_element_type=F32)

    block = pl.BlockSpec((1, 1, rows, columns), lambda i, *_: (i + first, 0, 0, 0))
    return pl.pallas_call(
        kernel,
        out_shape=jax.ShapeDtypeStruct(out.shape, F32),
        grid_spec=pltpu.PrefetchScalarGridSpec(
            num_scalar_prefetch=1,
            grid=(blocks,),
            in_specs=[pl.BlockSpec((width, columns), lambda i, place: (place[0], 0))]
            + [pl.BlockSpec((1, rows, width), lambda i, *_, offset=offset: (i + offset, 0, 0)) for offset in offsets]
            + [block],
            out_specs=block,
        ),
        input_output_aliases={2 + count: 0},
        compiler_params=pltpu.CompilerParams(vmem_limit_bytes=48 << 20),
        cost_estimate=pl.CostEstimate(
            flops=6 * blocks * rows * width * columns,
            bytes_accessed=4 * blocks * rows * (width + 2 * columns),
            transcendentals=0,
        ),
        name="finish",
    )(place, y, *piece, out)


def over_row(block, size):
    codes, held = [0], [block]
    bit = size // 2
    while bit:
        pairs = [(n, n ^ bit) for n in range(size)]
        held = held + [lax.ppermute(value, "row", pairs) for value in held]
        codes = codes + [code ^ bit for code in codes]
        bit //= 2
    return codes, held


def after(value, *others):
    return lax.optimization_barrier((value, *others))[0]


def body(right_sides, factor):
    row_count, real_count = lax.axis_size("row"), lax.axis_size("real")
    position = lax.axis_index("row")[None]
    mine = factor[:, 0]
    if real_count != 8:
        codes, sides = over_row(right_sides[0, 0], row_count)
        head = lax.all_gather(mine[0], "real", axis=1, tiled=True)
        codes, heads = over_row(head[None], row_count)
        y = solve(position, codes, [[part] for part in heads], jnp.zeros((1,), jnp.int32), sides)
        rest = lax.all_gather(mine[1:], "real", axis=2, tiled=True)
        return update(y, position, jnp.zeros((1,), jnp.int32), [[rest]], right_sides, 1, with_head=True)

    lanes = 2
    here = lax.axis_index("real")
    z, side = here // lanes, here % lanes
    outer = (z == 0) | (z == 3)
    pick = lambda a, b: jnp.where(outer, a, b)
    mirror = 3 - z
    partner = z ^ 1
    other = mirror ^ 1
    spot = lambda at, which: at * lanes + which

    def hop(value, bits):
        return lax.ppermute(value, "real", [(n, n ^ bits) for n in range(real_count)])

    def move(value, pairs):
        return lax.ppermute(value, "real", [(a * lanes + n, b * lanes + n) for a, b in pairs for n in range(lanes)])

    ends = lambda value: hop(value, 2)
    lane = lambda value: hop(value, 1)
    middle = lambda value: move(value, [(1, 2), (2, 1)])
    out = lambda value: move(value, [(1, 0), (2, 3)])
    outer_lane = lambda value: lax.ppermute(value, "real", [(n, n ^ 1) for n in (0, 1, 6, 7)])

    trailing = mine.shape[0] - 1
    cut = 1 + (trailing + 1) // 2
    own = mine[1:]
    halves = [slice(0, cut - 1), slice(cut - 1, trailing)]

    h_own = mine[0:1]
    h_line = [h_own] + [hop(h_own, bits) for bits in (2, 4, 6)]
    s1 = [lane(own[halves[0]]), None]
    h_line = jnp.concatenate(h_line)
    start = after(own, h_line)
    e1, m1 = ends(start), middle(start)
    h_all = jnp.concatenate([h_line, lane(h_line)])
    s1[1] = lane(after(own[halves[1]], s1[0]))
    s1 = jnp.concatenate(s1)
    owners = jnp.stack([here ^ bits for bits in (0, 2, 4, 6, 1, 3, 5, 7)]).astype(jnp.int32)
    codes, sides = over_row(after(right_sides, h_line)[0, 0], row_count)
    codes, heads = over_row(h_all, row_count)

    held = (e1, m1, s1)
    o2, m2, s2 = out(after(m1, *held)), middle(after(e1, *held)), lane(after(e1, *held))
    held = (o2, m2, s2)
    o3, m3, s3 = out(after(m2, *held)), middle(after(s1, *held)), lane(after(pick(o2, m2), *held))
    heads[0] = after(heads[0], *held)
    y = solve(position, codes, [[part] for part in heads], owners, sides)
    last = [outer_lane(after(o3[halves[0]], y)), out(after(s3[halves[1]], y))]

    places = [
        here,
        spot(partner, side),
        spot(z, 1 - side),
        pick(spot(other, side), spot(mirror, side)),
        spot(partner, 1 - side),
        pick(spot(mirror, side), spot(other, side)),
        spot(other, 1 - side),
    ]
    places = jnp.stack(places).astype(jnp.int32)
    pieces = [[own], [e1], [s1], [m1, o2], [s2], [m2, o3], [s3]]
    result = update(y, position, places, pieces, right_sides, 1, with_head=True)
    place = spot(mirror, 1 - side)[None].astype(jnp.int32)
    for k, first in ((1, cut), (0, 1)):
        result = finish(y, place, [(m3, first - 1), (last[k], 0)], result, first)
    return result


def solution(mesh):
    placed = (P(None, "row", None, "real"), P(None, "row", None, "real"))
    return jax.shard_map(
        body, mesh=mesh, in_specs=placed, out_specs=P(None, "row", None, "real"), check_vma=False
    )
```

```python
import functools
import math

import jax
import jax.numpy as jnp
from jax import lax
from jax.experimental import pallas as pl
from jax.experimental.pallas import tpu as pltpu
from jax.sharding import PartitionSpec as P

F32, BF16 = jnp.float32, jnp.bfloat16
TILE, HALF, BASE = 128, 64, 16


def split(value):
    high = value.astype(BF16)
    return high, (value - high.astype(F32)).astype(BF16)


def product(a_high, a_low, b_high, b_low):
    dot = functools.partial(jnp.dot, preferred_element_type=F32)
    return dot(a_high, b_high) + (dot(a_high, b_low) + dot(a_low, b_high))


def exact(a, b):
    return jnp.dot(a, b, precision=lax.Precision.HIGHEST, preferred_element_type=F32)


def half_inverses(tiles):
    count = len(tiles)
    lane = lax.broadcasted_iota(jnp.int32, (BASE, TILE), 1)
    row = lax.broadcasted_iota(jnp.int32, (BASE, TILE), 0)
    packed = []
    for tile in tiles:
        kept = jnp.zeros((BASE, TILE), F32)
        for g in range(TILE // BASE):
            kept = jnp.where(lane // BASE == g, tile[g * BASE : (g + 1) * BASE], kept)
        packed.append(kept)
    packed = jnp.concatenate(packed, axis=0)
    k = lax.broadcasted_iota(jnp.int32, (TILE, TILE), 0)
    m = lax.broadcasted_iota(jnp.int32, (TILE, TILE), 1)
    x = jnp.broadcast_to((row == lane % BASE).astype(F32)[None], (count, BASE, TILE))
    for j in range(BASE):
        spread = (k == (m // BASE) * BASE + j).astype(F32)
        column = exact(packed, spread).reshape(count, BASE, TILE)
        solved = x[:, j : j + 1] / column[:, j : j + 1]
        x = jnp.where(row[None] == j, solved, x - column * solved)
    inverses = []
    for t, tile in enumerate(tiles):
        w = jnp.where(k // BASE == m // BASE, jnp.concatenate([x[t]] * (TILE // BASE), axis=0), 0.0)
        size = BASE
        while size < HALF:
            joined = (k // (2 * size) == m // (2 * size)) & (k // size != m // size)
            w = w - exact(exact(w, jnp.where(joined, tile, 0.0)), w)
            size *= 2
        inverses.append(w)
    return inverses


def solve_kernel(codes, counts, place, head_refs, side_refs, y_ref, out_ref, l_high, l_low, y_high, y_low, landing, head_sems, side_sems):
    rows, width = head_refs[0].shape[-2:]
    window = l_high.shape[0]
    per_row = len(head_refs) // len(codes)
    head_copies, side_copies = [], []
    for c, code in enumerate(codes):
        at = pl.ds(pl.multiple_of((place[0] ^ code) * rows, rows), rows)
        begin = c * sum(counts)
        for p in range(per_row):
            n = c * per_row + p
            into = landing.at[begin : begin + counts[p]]
            head_copies.append(pltpu.make_async_copy(head_refs[n], into, head_sems.at[n]))
            begin += counts[p]
        side_copies.append(pltpu.make_async_copy(side_refs[c], y_ref.at[at], side_sems.at[c]))
    for copy in head_copies + side_copies:
        copy.start()
    for c, code in enumerate(codes):
        at = pl.ds(pl.multiple_of((place[0] ^ code) * rows, rows), rows)
        n = c * sum(counts)
        for p in range(per_row):
            head_copies[c * per_row + p].wait()
            for k in range(counts[p]):
                across = pl.ds(pl.multiple_of(place[1 + n] * width, width), width)
                high, low = split(landing[n])
                l_high[at, across] = high
                l_low[at, across] = low
                n += 1
    for copy in side_copies:
        copy.wait()
    tiles = []
    for t in range(window // TILE):
        at = slice(t * TILE, (t + 1) * TILE)
        tiles.append(l_high[at, at].astype(F32) + l_low[at, at].astype(F32))
    inverses = half_inverses(tiles)
    for t in range(window // TILE):
        begin = t * TILE
        value = y_ref[begin : begin + TILE]
        if t:
            value = value - product(
                l_high[begin : begin + TILE, :begin],
                l_low[begin : begin + TILE, :begin],
                y_high[:begin],
                y_low[:begin],
            )
        w = inverses[t]
        for h in range(TILE // HALF):
            part = value[h * HALF : (h + 1) * HALF]
            at = slice(begin + h * HALF, begin + (h + 1) * HALF)
            if h:
                inside = slice(begin, begin + h * HALF)
                part = part - product(
                    l_high[at, inside], l_low[at, inside], y_high[inside], y_low[inside]
                )
            inv = w[h * HALF : (h + 1) * HALF, h * HALF : (h + 1) * HALF]
            answer = product(*split(inv), *split(part))
            y_ref[at] = answer
            high, low = split(answer)
            y_high[at] = high
            y_low[at] = low
    at = pl.ds(pl.multiple_of(place[0] * rows, rows), rows)
    copy = pltpu.make_async_copy(y_ref.at[at], out_ref.at[0, 0], side_sems.at[0])
    copy.start()
    copy.wait()


def solve(position, codes, heads, owners, sides, out_shape):
    counts = [part.shape[0] for part in heads[0]]
    window = sum(counts) * heads[0][0].shape[-1]
    columns = sides[0].shape[-1]
    flat = [part for parts in heads for part in parts]
    total = len(flat)
    place = jnp.concatenate([position] + [owners] * len(codes))

    def kernel(place, *refs):
        head_refs, side_refs = refs[:total], refs[total : total + len(codes)]
        solve_kernel(codes, counts, place, head_refs, side_refs, *refs[total + len(codes) :])

    return pl.pallas_call(
        kernel,
        out_shape=[jax.ShapeDtypeStruct((window, columns), F32), jax.ShapeDtypeStruct(out_shape, F32)],
        in_specs=[pl.BlockSpec(memory_space=pltpu.SMEM)] + [pl.BlockSpec(memory_space=pl.ANY)] * (total + len(codes)),
        out_specs=[pl.BlockSpec(memory_space=pltpu.VMEM), pl.BlockSpec(memory_space=pl.ANY)],
        scratch_shapes=[
            pltpu.VMEM((window, window), BF16),
            pltpu.VMEM((window, window), BF16),
            pltpu.VMEM((window, columns), BF16),
            pltpu.VMEM((window, columns), BF16),
            pltpu.VMEM((len(codes) * sum(counts), *flat[0].shape[1:]), F32),
            pltpu.SemaphoreType.DMA((total,)),
            pltpu.SemaphoreType.DMA((len(codes),)),
        ],
        compiler_params=pltpu.CompilerParams(vmem_limit_bytes=48 << 20),
        cost_estimate=pl.CostEstimate(
            flops=30 * window * window * columns, bytes_accessed=4 * window * (window + 2 * columns), transcendentals=0
        ),
        name="solve",
    )(place, *flat, *sides)


def row_blocks(count):
    return next(n for n in (3, 2, 1) if count % n == 0)


def laid(parts, step, width):
    begins = [sum(part.shape[0] for part in parts[:n]) // step for n in range(len(parts))]
    ends = [begin + part.shape[0] // step for begin, part in zip(begins, parts)]

    def spec(part, begin, end):
        return pl.BlockSpec((step, part.shape[1], width), lambda i, *_: (jnp.clip(i - begin, 0, end - begin - 1), 0, 0))

    def read(refs, n):
        value = refs[0][n]
        for ref, begin in zip(refs[1:], begins[1:]):
            value = jnp.where(pl.program_id(0) >= begin, ref[n], value)
        return value

    return [spec(*given) for given in zip(parts, begins, ends)], read


def update(y, places, pieces, base, target=None):
    flat = [part if isinstance(part, tuple) else (part,) for piece in pieces for part in piece]
    blocks = sum(part.shape[0] for part in flat[0])
    rows = flat[0][0].shape[1]
    columns = y.shape[1]
    widths = [(piece[0][0] if isinstance(piece[0], tuple) else piece[0]).shape[-1] for piece in pieces]
    owner = [n for n, piece in enumerate(pieces) for _ in piece]
    depth = sum(widths)
    step = row_blocks(math.gcd(*(part.shape[0] for parts in flat for part in parts)))
    specs, reads = zip(*(laid(parts, step, widths[n]) for parts, n in zip(flat, owner)))
    lengths = [len(parts) for parts in flat]
    count = sum(lengths)

    def kernel(place, *refs):
        y_ref, base_ref = refs[0], refs[1]
        out_ref, y_high, y_low = refs[-3:]

        @pl.when(pl.program_id(0) == 0)
        def _():
            at = 0
            for n, width in enumerate(widths):
                high, low = split(y_ref[pl.ds(pl.multiple_of(place[n] * width, width), width)])
                y_high[at : at + width] = high
                y_low[at : at + width] = low
                at += width

        for n in range(step):
            wide = [0] * len(pieces)
            at = 2
            for read, length, piece in zip(reads, lengths, owner):
                wide[piece] = wide[piece] + read(refs[at : at + length], n)
                at += length
            high, low = split(jnp.concatenate(wide, axis=1))
            out_ref[n, 0] = base_ref[n, 0] - product(high, low, y_high[...], y_low[...])

    block = pl.BlockSpec(
        tuple(pl.Element(n) for n in (step, 1, rows, columns)), lambda i, *_: (i * step + 1, 0, 0, 0)
    )
    return pl.pallas_call(
        kernel,
        out_shape=jax.ShapeDtypeStruct(base.shape, F32),
        grid_spec=pltpu.PrefetchScalarGridSpec(
            num_scalar_prefetch=1,
            grid=(blocks // step,),
            in_specs=[pl.BlockSpec(y.shape, lambda i, *_: (0, 0)), block]
            + [spec for part in specs for spec in part]
            + [pl.BlockSpec(memory_space=pl.ANY)] * (target is not None),
            out_specs=block,
            scratch_shapes=[pltpu.VMEM((depth, columns), BF16), pltpu.VMEM((depth, columns), BF16)],
        ),
        input_output_aliases={2 if target is None else 3 + count: 0},
        compiler_params=pltpu.CompilerParams(vmem_limit_bytes=48 << 20),
        cost_estimate=pl.CostEstimate(
            flops=6 * blocks * rows * depth * columns,
            bytes_accessed=4 * blocks * rows * (depth + 2 * columns),
            transcendentals=0,
        ),
        name="update",
    )(places, y, base, *(part for parts in flat for part in parts), *([] if target is None else [target]))


def over_row(block, size):
    codes, held = [0], [block]
    bit = size // 2
    while bit:
        pairs = [(n, n ^ bit) for n in range(size)]
        held = held + [lax.ppermute(value, "row", pairs) for value in held]
        codes = codes + [code ^ bit for code in codes]
        bit //= 2
    return codes, held


def after(value, *others):
    return lax.optimization_barrier((value, *others))[0]


def body(right_sides, factor):
    row_count, real_count = lax.axis_size("row"), lax.axis_size("real")
    position = lax.axis_index("row")[None]
    mine = factor[:, 0]
    if real_count != 8:
        codes, sides = over_row(right_sides[0, 0], row_count)
        head = lax.all_gather(mine[0], "real", axis=1, tiled=True)
        codes, heads = over_row(head[None], row_count)
        whole = jnp.zeros((1,), jnp.int32)
        y, result = solve(position, codes, [[part] for part in heads], whole, sides, right_sides.shape)
        rest = lax.all_gather(mine[1:], "real", axis=2, tiled=True)
        return update(y, whole, [[rest]], right_sides, result)

    lanes = 2
    here = lax.axis_index("real")
    z, side = here // lanes, here % lanes
    outer = (z == 0) | (z == 3)
    pick = lambda a, b: jnp.where(outer, a, b)
    mirror = 3 - z
    partner = z ^ 1
    other = mirror ^ 1
    spot = lambda at, which: at * lanes + which

    def hop(value, bits):
        return lax.ppermute(value, "real", [(n, n ^ bits) for n in range(real_count)])

    def move(value, pairs):
        return lax.ppermute(value, "real", [(a * lanes + n, b * lanes + n) for a, b in pairs for n in range(lanes)])

    ends = lambda value: hop(value, 2)
    lane = lambda value: hop(value, 1)
    middle = lambda value: move(value, [(1, 2), (2, 1)])
    out = lambda value: move(value, [(1, 0), (2, 3)])

    trailing = mine.shape[0] - 1
    cut = trailing - trailing // 3
    own = mine[1:]
    halves = [slice(0, cut), slice(cut, trailing)]

    h_own = mine[0:1]
    h_line = [h_own] + [hop(h_own, bits) for bits in (2, 4, 6)]
    middle_row = (trailing + 1) // 2
    s1 = [lane(own[:middle_row]), None]
    start = after(own, h_line[1])
    e1, m1 = ends(start), middle(start)
    h_line = jnp.concatenate(h_line)
    h_all = jnp.concatenate([h_line, lane(h_line)])
    s1[1] = lane(after(own[middle_row:], s1[0]))
    s1 = jnp.concatenate(s1)
    owners = jnp.stack([here ^ bits for bits in (0, 2, 4, 6, 1, 3, 5, 7)]).astype(jnp.int32)
    codes, sides = over_row(right_sides[0, 0], row_count)
    codes, heads = over_row(h_all, row_count)

    o2, m2 = out(after(m1, e1)), middle(after(e1, m1, sides[1]))
    s2 = lane(after(e1, s1))
    first, second = halves
    o3 = out(after(m2, o2))
    both = after(pick(o2, m2), s2)
    s3 = [lane(both[first]), None]
    heads[0] = after(heads[0], o2, m2)
    y, result = solve(position, codes, [[part] for part in heads], owners, sides, right_sides.shape)
    s3[1] = lane(after(both[second], y))
    last = [ends(after(s3[0], y)), lane(pick(o3[second], m1[second]))]

    near_y = [
        here,
        spot(partner, side),
        spot(z, 1 - side),
        pick(spot(other, side), spot(mirror, side)),
        spot(partner, 1 - side),
    ]
    far_y = [pick(spot(mirror, side), spot(other, side)), spot(other, 1 - side), spot(mirror, 1 - side)]
    near_y, far_y = (jnp.stack(places).astype(jnp.int32) for places in (near_y, far_y))
    result = update(y, near_y, [[own], [e1], [s1], [m1, o2], [s2]], right_sides, result)
    return update(y, far_y, [[m2, o3], [tuple(s3)], [tuple(last)]], result)


def solution(mesh):
    placed = (P(None, "row", None, "real"), P(None, "row", None, "real"))
    return jax.shard_map(
        body, mesh=mesh, in_specs=placed, out_specs=P(None, "row", None, "real"), check_vma=False
    )
```

```python
import functools
import math

import jax
import jax.numpy as jnp
from jax import lax
from jax.experimental import pallas as pl
from jax.experimental.pallas import tpu as pltpu
from jax.sharding import PartitionSpec as P

F32, BF16 = jnp.float32, jnp.bfloat16
TILE, HALF, BASE = 128, 64, 16


def split(value):
    high = value.astype(BF16)
    return high, (value - high.astype(F32)).astype(BF16)


def product(a_high, a_low, b_high, b_low):
    wide = jnp.concatenate([a_high, a_low, a_high], axis=1)
    tall = jnp.concatenate([b_high, b_high, b_low], axis=0)
    return jnp.dot(wide, tall, preferred_element_type=F32)


def half_inverses(tiles):
    count = len(tiles)
    lane = lax.broadcasted_iota(jnp.int32, (BASE, TILE), 1)
    row = lax.broadcasted_iota(jnp.int32, (BASE, TILE), 0)
    packed = []
    for tile in tiles:
        kept = jnp.zeros((BASE, TILE), F32)
        for g in range(TILE // BASE):
            kept = jnp.where(lane // BASE == g, tile[g * BASE : (g + 1) * BASE], kept)
        packed.append(kept)
    packed = jnp.concatenate(packed, axis=0)
    k = lax.broadcasted_iota(jnp.int32, (TILE, TILE), 0)
    m = lax.broadcasted_iota(jnp.int32, (TILE, TILE), 1)
    high, rest = split(packed)
    middle = (packed - high.astype(F32) - rest.astype(F32)).astype(BF16)
    parts = jnp.concatenate([high, rest, middle], axis=1)
    columns = []
    for j in range(BASE):
        spread = (k == (m // BASE) * BASE + j).astype(F32).astype(BF16)
        tall = jnp.concatenate([spread] * 3, axis=0)
        columns.append(jnp.dot(parts, tall, preferred_element_type=F32).reshape(count, BASE, TILE))
    diagonal = columns[0]
    for j in range(1, BASE):
        diagonal = jnp.where(row[None] == j, columns[j], diagonal)
    scale = 1.0 / diagonal
    x = jnp.where((row == lane % BASE)[None], scale, 0.0)
    for j in range(BASE - 1):
        x = x - jnp.where(row[None] > j, columns[j] * scale, 0.0) * x[:, j : j + 1]
    inverses = [
        jnp.where(k // BASE == m // BASE, jnp.concatenate([x[t]] * (TILE // BASE), axis=0), 0.0) for t in range(count)
    ]
    size = BASE
    while size < HALF:
        joined = (k // (2 * size) == m // (2 * size)) & (k // size != m // size)
        halves = [split(w) for w in inverses]
        crossed = [product(*w, *split(jnp.where(joined, tile, 0.0))) for w, tile in zip(halves, tiles)]
        inverses = [w - product(*split(c), *h) for w, c, h in zip(inverses, crossed, halves)]
        size *= 2
    return inverses


def solve_kernel(codes, counts, place, head_refs, side_refs, y_ref, out_ref, l_high, l_low, y_high, y_low, landing, head_sems, side_sems):
    rows, width = head_refs[0].shape[-2:]
    window = l_high.shape[0]
    per_row = len(head_refs) // len(codes)
    head_copies, side_copies = [], []
    for c, code in enumerate(codes):
        at = pl.ds(pl.multiple_of((place[0] ^ code) * rows, rows), rows)
        begin = c * sum(counts)
        for p in range(per_row):
            n = c * per_row + p
            into = landing.at[begin : begin + counts[p]]
            head_copies.append(pltpu.make_async_copy(head_refs[n], into, head_sems.at[n]))
            begin += counts[p]
        side_copies.append(pltpu.make_async_copy(side_refs[c], y_ref.at[at], side_sems.at[c]))
    for copy in head_copies + side_copies:
        copy.start()
    for c, code in enumerate(codes):
        at = pl.ds(pl.multiple_of((place[0] ^ code) * rows, rows), rows)
        n = c * sum(counts)
        for p in range(per_row):
            head_copies[c * per_row + p].wait()
            for k in range(counts[p]):
                across = pl.ds(pl.multiple_of(place[1 + n] * width, width), width)
                high, low = split(landing[n])
                l_high[at, across] = high
                l_low[at, across] = low
                n += 1
    for copy in side_copies:
        copy.wait()
    tiles = []
    for t in range(window // TILE):
        at = slice(t * TILE, (t + 1) * TILE)
        tiles.append(l_high[at, at].astype(F32) + l_low[at, at].astype(F32))
    inverses = half_inverses(tiles)
    ready = y_ref[:TILE]
    for t in range(window // TILE):
        begin = t * TILE
        value = ready
        if t:
            before = slice(begin - TILE, begin)
            at = slice(begin, begin + TILE)
            value = value - product(l_high[at, before], l_low[at, before], *solved)
        w = inverses[t]
        answers = []
        for h in range(TILE // HALF):
            part = value[h * HALF : (h + 1) * HALF]
            at = slice(begin + h * HALF, begin + (h + 1) * HALF)
            if h:
                inside = slice(begin, begin + h * HALF)
                part = part - product(l_high[at, inside], l_low[at, inside], *answers[0])
            inv = w[h * HALF : (h + 1) * HALF, h * HALF : (h + 1) * HALF]
            answer = product(*split(inv), *split(part))
            y_ref[at] = answer
            answers.append(split(answer))
            if h == 0 and begin + TILE < window:
                following = slice(begin + TILE, begin + 2 * TILE)
                ready = y_ref[following]
                if t:
                    ready = ready - product(
                        l_high[following, :begin], l_low[following, :begin], y_high[:begin], y_low[:begin]
                    )
        solved = [jnp.concatenate(both, axis=0) for both in zip(*answers)]
        y_high[begin : begin + TILE], y_low[begin : begin + TILE] = solved
    at = pl.ds(pl.multiple_of(place[0] * rows, rows), rows)
    copy = pltpu.make_async_copy(y_ref.at[at], out_ref.at[0, 0], side_sems.at[0])
    copy.start()
    copy.wait()


def solve(position, codes, heads, owners, sides, out_shape):
    counts = [part.shape[0] for part in heads[0]]
    window = sum(counts) * heads[0][0].shape[-1]
    columns = sides[0].shape[-1]
    flat = [part for parts in heads for part in parts]
    total = len(flat)
    place = jnp.concatenate([position] + [owners] * len(codes))

    def kernel(place, *refs):
        head_refs, side_refs = refs[:total], refs[total : total + len(codes)]
        solve_kernel(codes, counts, place, head_refs, side_refs, *refs[total + len(codes) :])

    return pl.pallas_call(
        kernel,
        out_shape=[jax.ShapeDtypeStruct((window, columns), F32), jax.ShapeDtypeStruct(out_shape, F32)],
        in_specs=[pl.BlockSpec(memory_space=pltpu.SMEM)] + [pl.BlockSpec(memory_space=pl.ANY)] * (total + len(codes)),
        out_specs=[pl.BlockSpec(memory_space=pltpu.VMEM), pl.BlockSpec(memory_space=pl.ANY)],
        scratch_shapes=[
            pltpu.VMEM((window, window), BF16),
            pltpu.VMEM((window, window), BF16),
            pltpu.VMEM((window, columns), BF16),
            pltpu.VMEM((window, columns), BF16),
            pltpu.VMEM((len(codes) * sum(counts), *flat[0].shape[1:]), F32),
            pltpu.SemaphoreType.DMA((total,)),
            pltpu.SemaphoreType.DMA((len(codes),)),
        ],
        compiler_params=pltpu.CompilerParams(vmem_limit_bytes=48 << 20),
        cost_estimate=pl.CostEstimate(
            flops=30 * window * window * columns, bytes_accessed=4 * window * (window + 2 * columns), transcendentals=0
        ),
        name="solve",
    )(place, *flat, *sides)


def load(places, begin, widths, y_ref, y_high, y_low):
    at = 0
    for n, width in enumerate(widths):
        high, low = split(y_ref[pl.ds(pl.multiple_of(places[begin + n] * width, width), width)])
        y_high[at : at + width] = high
        y_low[at : at + width] = low
        at += width


def update_first(y, places, pieces, base):
    flat = [part for piece in pieces for part in piece]
    blocks, rows, _ = flat[0].shape
    columns = y.shape[1]
    widths = [piece[0].shape[-1] for piece in pieces]
    count, depth = len(flat), sum(widths)
    step = next(n for n in (3, 2, 1) if blocks % n == 0)

    def kernel(place, y_ref, base_ref, *refs):
        piece_refs, (acc_ref, y_high, y_low, done) = refs[:count], refs[count:]
        load(place, 0, widths, y_ref, y_high, y_low)
        done[0] = 0

        def body(base_block, *piece_blocks):
            for n in range(step):
                parts = iter(piece_blocks)
                wide = [sum(next(parts)[n] for _ in piece) for piece in pieces]
                high, low = split(jnp.concatenate(wide, axis=1))
                value = base_block[n, 0] - product(high, low, y_high[...], y_low[...])
                acc_ref[done[0] + n] = value
            done[0] += step

        pltpu.emit_pipeline(
            body,
            grid=(blocks // step,),
            in_specs=[pl.BlockSpec((step, 1, rows, columns), lambda i: (i, 0, 0, 0))]
            + [pl.BlockSpec((step, rows, part.shape[-1]), lambda i: (i, 0, 0)) for part in flat],
        )(base_ref.at[pl.ds(1, blocks)], *piece_refs)

    anywhere = pl.BlockSpec(memory_space=pl.ANY)
    inside = pl.BlockSpec(memory_space=pltpu.VMEM)
    return pl.pallas_call(
        kernel,
        out_shape=jax.ShapeDtypeStruct((blocks, rows, columns), F32),
        in_specs=[pl.BlockSpec(memory_space=pltpu.SMEM), inside] + [anywhere] * (1 + count),
        out_specs=inside,
        scratch_shapes=[
            pltpu.VMEM((depth, columns), BF16),
            pltpu.VMEM((depth, columns), BF16),
            pltpu.SMEM((1,), jnp.int32),
        ],
        compiler_params=pltpu.CompilerParams(vmem_limit_bytes=44 << 20),
        cost_estimate=pl.CostEstimate(
            flops=6 * blocks * rows * depth * columns,
            bytes_accessed=4 * blocks * rows * (depth + 2 * columns),
            transcendentals=0,
        ),
        name="update_first",
    )(places, y, base, *flat)


def update_last(y, places, pieces, acc, target):
    flat = [part for piece in pieces for laid in piece for part in laid]
    blocks, rows, columns = acc.shape
    widths = [piece[0][0].shape[-1] for piece in pieces]
    count, depth = len(flat), sum(widths)

    def kernel(place, y_ref, acc_ref, *refs):
        piece_refs = refs[:count]
        out_ref, y_high, y_low, done, sems = refs[count + 1 :]
        load(place, 0, widths, y_ref, y_high, y_low)
        copies = []
        for i in range(blocks):
            at, wide = 0, []
            for piece in pieces:
                value = 0
                for laid in piece:
                    begin = 0
                    for part in laid:
                        if begin <= i < begin + part.shape[0]:
                            value = value + piece_refs[at][i - begin]
                        begin += part.shape[0]
                        at += 1
                wide.append(value)
            high, low = split(jnp.concatenate(wide, axis=1))
            done[i] = acc_ref[i] - product(high, low, y_high[...], y_low[...])
            copies.append(pltpu.make_async_copy(done.at[i], out_ref.at[i + 1, 0], sems.at[i]))
            copies[-1].start()
        for copy in copies:
            copy.wait()

    anywhere = pl.BlockSpec(memory_space=pl.ANY)
    inside = pl.BlockSpec(memory_space=pltpu.VMEM)
    return pl.pallas_call(
        kernel,
        out_shape=jax.ShapeDtypeStruct(target.shape, F32),
        in_specs=[pl.BlockSpec(memory_space=pltpu.SMEM)] + [inside] * (2 + count) + [anywhere],
        out_specs=anywhere,
        scratch_shapes=[
            pltpu.VMEM((depth, columns), BF16),
            pltpu.VMEM((depth, columns), BF16),
            pltpu.VMEM((blocks, rows, columns), F32),
            pltpu.SemaphoreType.DMA((blocks,)),
        ],
        input_output_aliases={3 + count: 0},
        compiler_params=pltpu.CompilerParams(vmem_limit_bytes=44 << 20),
        cost_estimate=pl.CostEstimate(
            flops=6 * blocks * rows * depth * columns,
            bytes_accessed=4 * blocks * rows * (depth + 2 * columns),
            transcendentals=0,
        ),
        name="update_last",
    )(places, y, acc, *flat, target)


def over_row(block, size):
    codes, held = [0], [block]
    bit = size // 2
    while bit:
        pairs = [(n, n ^ bit) for n in range(size)]
        held = held + [lax.ppermute(value, "row", pairs) for value in held]
        codes = codes + [code ^ bit for code in codes]
        bit //= 2
    return codes, held


def after(value, *others):
    return lax.optimization_barrier((value, *others))[0]


def body(right_sides, factor):
    row_count, real_count = lax.axis_size("row"), lax.axis_size("real")
    position = lax.axis_index("row")[None]
    mine = factor[:, 0]
    if real_count != 8:
        codes, sides = over_row(right_sides[0, 0], row_count)
        head = lax.all_gather(mine[0], "real", axis=1, tiled=True)
        codes, heads = over_row(head[None], row_count)
        whole = jnp.zeros((1,), jnp.int32)
        y, result = solve(position, codes, [[part] for part in heads], whole, sides, right_sides.shape)
        rest = lax.all_gather(mine[1:], "real", axis=2, tiled=True)
        half = rest.shape[2] // 2
        acc = update_first(y, whole, [[rest[:, :, :half]]], right_sides)
        return update_last(y, whole + 1, [[[rest[:, :, half:]]]], acc, result)

    lanes = 2
    here = lax.axis_index("real")
    z, side = here // lanes, here % lanes
    outer = (z == 0) | (z == 3)
    pick = lambda a, b: jnp.where(outer, a, b)
    mirror = 3 - z
    partner = z ^ 1
    other = mirror ^ 1
    spot = lambda at, which: at * lanes + which

    def hop(value, bits):
        return lax.ppermute(value, "real", [(n, n ^ bits) for n in range(real_count)])

    def move(value, pairs):
        return lax.ppermute(value, "real", [(a * lanes + n, b * lanes + n) for a, b in pairs for n in range(lanes)])

    ends = lambda value: hop(value, 2)
    lane = lambda value: hop(value, 1)
    middle = lambda value: move(value, [(1, 2), (2, 1)])
    out = lambda value: move(value, [(1, 0), (2, 3)])

    trailing = mine.shape[0] - 1
    cut = (trailing + 1) // 2
    own = mine[1:]
    halves = [slice(0, cut), slice(cut, trailing)]

    h_own = mine[0:1]
    h_line = [h_own] + [hop(h_own, bits) for bits in (2, 4, 6)]
    middle_row = (trailing + 1) // 2
    s1 = [lane(own[:middle_row]), None]
    start = after(own, h_line[1])
    e1, m1 = ends(start), middle(start)
    far_head = h_line[2]
    h_line = jnp.concatenate(h_line)
    h_all = jnp.concatenate([h_line, lane(h_line)])
    s1[1] = lane(after(own[middle_row:], s1[0]))
    s1 = jnp.concatenate(s1)
    owners = jnp.stack([here ^ bits for bits in (0, 2, 4, 6, 1, 3, 5, 7)]).astype(jnp.int32)
    codes, sides = over_row(after(right_sides, far_head)[0, 0], row_count)
    codes, heads = over_row(after(h_all, sides[1]), row_count)

    first, second = halves
    o2 = out(after(m1, e1))
    m2 = middle(e1)
    s2 = lane(after(e1, s1))
    o3 = [out(m2[rows]) for rows in halves]
    both = [pick(o2, m2)[rows] for rows in halves]
    s3 = [lane(after(both[0], s2)), None]
    heads[0] = after(heads[0], o2, m2)
    y, result = solve(position, codes, [[part] for part in heads], owners, sides, right_sides.shape)
    s3[1] = lane(after(both[1], y))
    last = [ends(after(s3[0], y, o3[1])), lane(pick(o3[1], m1[second]))]

    near_y = [
        here,
        spot(partner, side),
        spot(z, 1 - side),
        pick(spot(other, side), spot(mirror, side)),
        spot(partner, 1 - side),
    ]
    far_y = [pick(spot(mirror, side), spot(other, side)), spot(other, 1 - side), spot(mirror, 1 - side)]
    near_y, far_y = (jnp.stack(places).astype(jnp.int32) for places in (near_y, far_y))
    acc = update_first(y, near_y, [[own], [e1], [s1], [m1, o2], [s2]], right_sides)
    return update_last(y, far_y, [[[m2], o3], [s3], [last]], acc, result)


def solution(mesh):
    placed = (P(None, "row", None, "real"), P(None, "row", None, "real"))
    return jax.shard_map(
        body, mesh=mesh, in_specs=placed, out_specs=P(None, "row", None, "real"), check_vma=False
    )
```

```python
import functools
import math

import jax
import jax.numpy as jnp
from jax import lax
from jax.experimental import pallas as pl
from jax.experimental.pallas import tpu as pltpu
from jax.sharding import PartitionSpec as P

F32, BF16 = jnp.float32, jnp.bfloat16
TILE, HALF, BASE = 128, 64, 16


def split(value):
    high = value.astype(BF16)
    return high, (value - high.astype(F32)).astype(BF16)


def product(a_high, a_low, b_high, b_low):
    wide = jnp.concatenate([a_high, a_low, a_high], axis=1)
    tall = jnp.concatenate([b_high, b_high, b_low], axis=0)
    return jnp.dot(wide, tall, preferred_element_type=F32)


def half_inverses(tiles):
    count = len(tiles)
    lane = lax.broadcasted_iota(jnp.int32, (BASE, TILE), 1)
    row = lax.broadcasted_iota(jnp.int32, (BASE, TILE), 0)
    packed = []
    for tile in tiles:
        kept = jnp.zeros((BASE, TILE), F32)
        for g in range(TILE // BASE):
            kept = jnp.where(lane // BASE == g, tile[g * BASE : (g + 1) * BASE], kept)
        packed.append(kept)
    packed = jnp.concatenate(packed, axis=0)
    k = lax.broadcasted_iota(jnp.int32, (TILE, TILE), 0)
    m = lax.broadcasted_iota(jnp.int32, (TILE, TILE), 1)
    high, rest = split(packed)
    middle = (packed - high.astype(F32) - rest.astype(F32)).astype(BF16)
    parts = jnp.concatenate([high, rest, middle], axis=1)
    columns = []
    for j in range(BASE):
        spread = (k == (m // BASE) * BASE + j).astype(F32).astype(BF16)
        tall = jnp.concatenate([spread] * 3, axis=0)
        columns.append(jnp.dot(parts, tall, preferred_element_type=F32).reshape(count, BASE, TILE))
    diagonal = columns[0]
    for j in range(1, BASE):
        diagonal = jnp.where(row[None] == j, columns[j], diagonal)
    scale = 1.0 / diagonal
    x = jnp.where((row == lane % BASE)[None], scale, 0.0)
    for j in range(BASE - 1):
        x = x - jnp.where(row[None] > j, columns[j] * scale, 0.0) * x[:, j : j + 1]
    inverses = [
        jnp.where(k // BASE == m // BASE, jnp.concatenate([x[t]] * (TILE // BASE), axis=0), 0.0) for t in range(count)
    ]
    size = BASE
    while size < HALF:
        joined = (k // (2 * size) == m // (2 * size)) & (k // size != m // size)
        halves = [split(w) for w in inverses]
        crossed = [product(*w, *split(jnp.where(joined, tile, 0.0))) for w, tile in zip(halves, tiles)]
        inverses = [w - product(*split(c), *h) for w, c, h in zip(inverses, crossed, halves)]
        size *= 2
    return inverses


def solve_kernel(codes, counts, place, head_refs, side_refs, y_ref, out_ref, l_high, l_low, y_high, y_low, landing, head_sems, side_sems):
    rows, width = head_refs[0].shape[-2:]
    window = l_high.shape[0]
    per_row = len(head_refs) // len(codes)
    head_copies, side_copies = [], []
    for c, code in enumerate(codes):
        at = pl.ds(pl.multiple_of((place[0] ^ code) * rows, rows), rows)
        begin = c * sum(counts)
        for p in range(per_row):
            n = c * per_row + p
            into = landing.at[begin : begin + counts[p]]
            head_copies.append(pltpu.make_async_copy(head_refs[n], into, head_sems.at[n]))
            begin += counts[p]
        side_copies.append(pltpu.make_async_copy(side_refs[c], y_ref.at[at], side_sems.at[c]))
    for copy in head_copies + side_copies:
        copy.start()
    for c, code in enumerate(codes):
        at = pl.ds(pl.multiple_of((place[0] ^ code) * rows, rows), rows)
        n = c * sum(counts)
        for p in range(per_row):
            head_copies[c * per_row + p].wait()
            for k in range(counts[p]):
                across = pl.ds(pl.multiple_of(place[1 + n] * width, width), width)
                high, low = split(landing[n])
                l_high[at, across] = high
                l_low[at, across] = low
                n += 1
    for copy in side_copies:
        copy.wait()
    tiles = []
    for t in range(window // TILE):
        at = slice(t * TILE, (t + 1) * TILE)
        tiles.append(l_high[at, at].astype(F32) + l_low[at, at].astype(F32))
    inverses = half_inverses(tiles)
    ready = y_ref[:TILE]
    for t in range(window // TILE):
        begin = t * TILE
        value = ready
        if t:
            before = slice(begin - TILE, begin)
            at = slice(begin, begin + TILE)
            value = value - product(l_high[at, before], l_low[at, before], *solved)
        w = inverses[t]
        answers = []
        for h in range(TILE // HALF):
            part = value[h * HALF : (h + 1) * HALF]
            at = slice(begin + h * HALF, begin + (h + 1) * HALF)
            if h:
                inside = slice(begin, begin + h * HALF)
                part = part - product(l_high[at, inside], l_low[at, inside], *answers[0])
            inv = w[h * HALF : (h + 1) * HALF, h * HALF : (h + 1) * HALF]
            answer = product(*split(inv), *split(part))
            y_ref[at] = answer
            answers.append(split(answer))
            if h == 0 and begin + TILE < window:
                following = slice(begin + TILE, begin + 2 * TILE)
                ready = y_ref[following]
                if t:
                    ready = ready - product(
                        l_high[following, :begin], l_low[following, :begin], y_high[:begin], y_low[:begin]
                    )
        solved = [jnp.concatenate(both, axis=0) for both in zip(*answers)]
        y_high[begin : begin + TILE], y_low[begin : begin + TILE] = solved
    at = pl.ds(pl.multiple_of(place[0] * rows, rows), rows)
    copy = pltpu.make_async_copy(y_ref.at[at], out_ref.at[0, 0], side_sems.at[0])
    copy.start()
    copy.wait()


def solve(position, codes, heads, owners, sides, out_shape):
    counts = [part.shape[0] for part in heads[0]]
    window = sum(counts) * heads[0][0].shape[-1]
    columns = sides[0].shape[-1]
    flat = [part for parts in heads for part in parts]
    total = len(flat)
    place = jnp.concatenate([position] + [owners] * len(codes))

    def kernel(place, *refs):
        head_refs, side_refs = refs[:total], refs[total : total + len(codes)]
        solve_kernel(codes, counts, place, head_refs, side_refs, *refs[total + len(codes) :])

    return pl.pallas_call(
        kernel,
        out_shape=[jax.ShapeDtypeStruct((window, columns), F32), jax.ShapeDtypeStruct(out_shape, F32)],
        in_specs=[pl.BlockSpec(memory_space=pltpu.SMEM)] + [pl.BlockSpec(memory_space=pl.ANY)] * (total + len(codes)),
        out_specs=[pl.BlockSpec(memory_space=pltpu.VMEM), pl.BlockSpec(memory_space=pl.ANY)],
        scratch_shapes=[
            pltpu.VMEM((window, window), BF16),
            pltpu.VMEM((window, window), BF16),
            pltpu.VMEM((window, columns), BF16),
            pltpu.VMEM((window, columns), BF16),
            pltpu.VMEM((len(codes) * sum(counts), *flat[0].shape[1:]), F32),
            pltpu.SemaphoreType.DMA((total,)),
            pltpu.SemaphoreType.DMA((len(codes),)),
        ],
        compiler_params=pltpu.CompilerParams(vmem_limit_bytes=48 << 20),
        cost_estimate=pl.CostEstimate(
            flops=30 * window * window * columns, bytes_accessed=4 * window * (window + 2 * columns), transcendentals=0
        ),
        name="solve",
    )(place, *flat, *sides)


def load(places, begin, widths, y_ref, y_high, y_low):
    at = 0
    for n, width in enumerate(widths):
        high, low = split(y_ref[pl.ds(pl.multiple_of(places[begin + n] * width, width), width)])
        y_high[at : at + width] = high
        y_low[at : at + width] = low
        at += width


def update_first(y, places, pieces, base):
    flat = [part for piece in pieces for part in piece]
    blocks, rows, _ = flat[0].shape
    columns = y.shape[1]
    widths = [piece[0].shape[-1] for piece in pieces]
    count, depth = len(flat), sum(widths)
    step = next(n for n in (3, 2, 1) if blocks % n == 0)

    def kernel(place, y_ref, base_ref, *refs):
        piece_refs, (acc_ref, y_high, y_low, done) = refs[:count], refs[count:]
        load(place, 0, widths, y_ref, y_high, y_low)
        done[0] = 0

        def body(base_block, *piece_blocks):
            for n in range(step):
                parts = iter(piece_blocks)
                wide = [sum(next(parts)[n] for _ in piece) for piece in pieces]
                high, low = split(jnp.concatenate(wide, axis=1))
                value = base_block[n, 0] - product(high, low, y_high[...], y_low[...])
                acc_ref[done[0] + n] = value
            done[0] += step

        pltpu.emit_pipeline(
            body,
            grid=(blocks // step,),
            in_specs=[pl.BlockSpec((step, 1, rows, columns), lambda i: (i, 0, 0, 0))]
            + [pl.BlockSpec((step, rows, part.shape[-1]), lambda i: (i, 0, 0)) for part in flat],
        )(base_ref.at[pl.ds(1, blocks)], *piece_refs)

    anywhere = pl.BlockSpec(memory_space=pl.ANY)
    inside = pl.BlockSpec(memory_space=pltpu.VMEM)
    return pl.pallas_call(
        kernel,
        out_shape=pltpu.VMEM((blocks, rows, columns), F32),
        in_specs=[pl.BlockSpec(memory_space=pltpu.SMEM), inside] + [anywhere] * (1 + count),
        out_specs=inside,
        scratch_shapes=[
            pltpu.VMEM((depth, columns), BF16),
            pltpu.VMEM((depth, columns), BF16),
            pltpu.SMEM((1,), jnp.int32),
        ],
        compiler_params=pltpu.CompilerParams(vmem_limit_bytes=44 << 20),
        cost_estimate=pl.CostEstimate(
            flops=6 * blocks * rows * depth * columns,
            bytes_accessed=4 * blocks * rows * (depth + 2 * columns),
            transcendentals=0,
        ),
        name="update_first",
    )(places, y, base, *flat)


def update_last(y, places, pieces, acc, target):
    flat = [part for piece in pieces for laid in piece for part in laid]
    blocks, rows, columns = acc.shape
    widths = [piece[0][0].shape[-1] for piece in pieces]
    count, depth = len(flat), sum(widths)

    def kernel(place, y_ref, acc_ref, *refs):
        piece_refs = refs[:count]
        out_ref, y_high, y_low, done, sems = refs[count + 1 :]
        load(place, 0, widths, y_ref, y_high, y_low)
        copies = []
        for i in range(blocks):
            at, wide = 0, []
            for piece in pieces:
                value = 0
                for laid in piece:
                    begin = 0
                    for part in laid:
                        if begin <= i < begin + part.shape[0]:
                            value = value + piece_refs[at][i - begin]
                        begin += part.shape[0]
                        at += 1
                wide.append(value)
            high, low = split(jnp.concatenate(wide, axis=1))
            done[i] = acc_ref[i] - product(high, low, y_high[...], y_low[...])
            copies.append(pltpu.make_async_copy(done.at[i], out_ref.at[i + 1, 0], sems.at[i]))
            copies[-1].start()
        for copy in copies:
            copy.wait()

    anywhere = pl.BlockSpec(memory_space=pl.ANY)
    inside = pl.BlockSpec(memory_space=pltpu.VMEM)
    return pl.pallas_call(
        kernel,
        out_shape=jax.ShapeDtypeStruct(target.shape, F32),
        in_specs=[pl.BlockSpec(memory_space=pltpu.SMEM)] + [inside] * (2 + count) + [anywhere],
        out_specs=anywhere,
        scratch_shapes=[
            pltpu.VMEM((depth, columns), BF16),
            pltpu.VMEM((depth, columns), BF16),
            pltpu.VMEM((blocks, rows, columns), F32),
            pltpu.SemaphoreType.DMA((blocks,)),
        ],
        input_output_aliases={3 + count: 0},
        compiler_params=pltpu.CompilerParams(vmem_limit_bytes=44 << 20),
        cost_estimate=pl.CostEstimate(
            flops=6 * blocks * rows * depth * columns,
            bytes_accessed=4 * blocks * rows * (depth + 2 * columns),
            transcendentals=0,
        ),
        name="update_last",
    )(places, y, pltpu.with_memory_space_constraint(acc, pltpu.VMEM), *flat, target)


def over_row(block, size):
    codes, held = [0], [block]
    bit = size // 2
    while bit:
        pairs = [(n, n ^ bit) for n in range(size)]
        held = held + [lax.ppermute(value, "row", pairs) for value in held]
        codes = codes + [code ^ bit for code in codes]
        bit //= 2
    return codes, held


def after(value, *others):
    return lax.optimization_barrier((value, *others))[0]


def body(right_sides, factor):
    row_count, real_count = lax.axis_size("row"), lax.axis_size("real")
    position = lax.axis_index("row")[None]
    mine = factor[:, 0]
    if real_count != 8:
        codes, sides = over_row(right_sides[0, 0], row_count)
        head = lax.all_gather(mine[0], "real", axis=1, tiled=True)
        codes, heads = over_row(head[None], row_count)
        whole = jnp.zeros((1,), jnp.int32)
        y, result = solve(position, codes, [[part] for part in heads], whole, sides, right_sides.shape)
        rest = lax.all_gather(mine[1:], "real", axis=2, tiled=True)
        half = rest.shape[2] // 2
        acc = update_first(y, whole, [[rest[:, :, :half]]], right_sides)
        return update_last(y, whole + 1, [[[rest[:, :, half:]]]], acc, result)

    lanes = 2
    here = lax.axis_index("real")
    z, side = here // lanes, here % lanes
    outer = (z == 0) | (z == 3)
    pick = lambda a, b: jnp.where(outer, a, b)
    mirror = 3 - z
    partner = z ^ 1
    other = mirror ^ 1
    spot = lambda at, which: at * lanes + which

    def hop(value, bits):
        return lax.ppermute(value, "real", [(n, n ^ bits) for n in range(real_count)])

    def move(value, pairs):
        return lax.ppermute(value, "real", [(a * lanes + n, b * lanes + n) for a, b in pairs for n in range(lanes)])

    ends = lambda value: hop(value, 2)
    lane = lambda value: hop(value, 1)
    middle = lambda value: move(value, [(1, 2), (2, 1)])
    out = lambda value: move(value, [(1, 0), (2, 3)])

    trailing = mine.shape[0] - 1
    cut = (trailing + 1) // 2
    own = mine[1:]
    halves = [slice(0, cut), slice(cut, trailing)]

    h_own = mine[0:1]
    h_line = [h_own] + [hop(h_own, bits) for bits in (2, 4, 6)]
    middle_row = (trailing + 1) // 2
    s1 = [lane(own[:middle_row]), None]
    start = after(own, h_line[1])
    e1, m1 = ends(start), middle(start)
    far_head = h_line[2]
    h_line = jnp.concatenate(h_line)
    h_all = jnp.concatenate([h_line, lane(h_line)])
    s1[1] = lane(after(own[middle_row:], s1[0]))
    s1 = jnp.concatenate(s1)
    owners = jnp.stack([here ^ bits for bits in (0, 2, 4, 6, 1, 3, 5, 7)]).astype(jnp.int32)
    codes, sides = over_row(after(right_sides, far_head)[0, 0], row_count)
    codes, heads = over_row(after(h_all, sides[1]), row_count)

    first, second = halves
    o2 = out(after(m1, e1))
    m2 = middle(e1)
    s2 = lane(after(e1, s1))
    o3 = [out(m2[rows]) for rows in halves]
    both = [pick(o2, m2)[rows] for rows in halves]
    s3 = [lane(after(both[0], s2)), None]
    heads[0] = after(heads[0], o2, m2)
    y, result = solve(position, codes, [[part] for part in heads], owners, sides, right_sides.shape)
    s3[1] = lane(after(both[1], y))
    last = [ends(after(s3[0], y, o3[1])), lane(pick(o3[1], m1[second]))]

    near_y = [
        here,
        spot(partner, side),
        spot(z, 1 - side),
        pick(spot(other, side), spot(mirror, side)),
        spot(partner, 1 - side),
    ]
    far_y = [pick(spot(mirror, side), spot(other, side)), spot(other, 1 - side), spot(mirror, 1 - side)]
    near_y, far_y = (jnp.stack(places).astype(jnp.int32) for places in (near_y, far_y))
    inside = lambda parts: [pltpu.with_memory_space_constraint(part, pltpu.VMEM) for part in parts]
    acc = update_first(y, near_y, [[own], [e1], [s1], [m1, o2], [s2]], right_sides)
    return update_last(y, far_y, [[[m2], o3], [s3], [inside(last)]], acc, result)


def solution(mesh):
    placed = (P(None, "row", None, "real"), P(None, "row", None, "real"))
    return jax.shard_map(
        body, mesh=mesh, in_specs=placed, out_specs=P(None, "row", None, "real"), check_vma=False
    )
```

```python
import functools
import math

import jax
import jax.numpy as jnp
from jax import lax
from jax.experimental import pallas as pl
from jax.experimental.pallas import tpu as pltpu
from jax.sharding import PartitionSpec as P

F32, BF16 = jnp.float32, jnp.bfloat16
TILE, HALF, BASE = 128, 64, 16


def split(value):
    high = value.astype(BF16)
    return high, (value - high.astype(F32)).astype(BF16)


def product(a_high, a_low, b_high, b_low):
    wide = jnp.concatenate([a_high, a_low, a_high], axis=1)
    tall = jnp.concatenate([b_high, b_high, b_low], axis=0)
    return jnp.dot(wide, tall, preferred_element_type=F32)


def half_inverses(tiles):
    count = len(tiles)
    lane = lax.broadcasted_iota(jnp.int32, (BASE, TILE), 1)
    row = lax.broadcasted_iota(jnp.int32, (BASE, TILE), 0)
    packed = []
    for tile in tiles:
        kept = jnp.zeros((BASE, TILE), F32)
        for g in range(TILE // BASE):
            kept = jnp.where(lane // BASE == g, tile[g * BASE : (g + 1) * BASE], kept)
        packed.append(kept)
    packed = jnp.concatenate(packed, axis=0)
    k = lax.broadcasted_iota(jnp.int32, (TILE, TILE), 0)
    m = lax.broadcasted_iota(jnp.int32, (TILE, TILE), 1)
    high, rest = split(packed)
    middle = (packed - high.astype(F32) - rest.astype(F32)).astype(BF16)
    parts = jnp.concatenate([high, rest, middle], axis=1)
    columns = []
    for j in range(BASE):
        spread = (k == (m // BASE) * BASE + j).astype(F32).astype(BF16)
        tall = jnp.concatenate([spread] * 3, axis=0)
        columns.append(jnp.dot(parts, tall, preferred_element_type=F32).reshape(count, BASE, TILE))
    diagonal = columns[0]
    for j in range(1, BASE):
        diagonal = jnp.where(row[None] == j, columns[j], diagonal)
    scale = 1.0 / diagonal
    x = jnp.where((row == lane % BASE)[None], scale, 0.0)
    for j in range(BASE - 1):
        x = x - jnp.where(row[None] > j, columns[j] * scale, 0.0) * x[:, j : j + 1]
    inverses = [
        jnp.where(k // BASE == m // BASE, jnp.concatenate([x[t]] * (TILE // BASE), axis=0), 0.0) for t in range(count)
    ]
    size = BASE
    while size < HALF:
        joined = (k // (2 * size) == m // (2 * size)) & (k // size != m // size)
        halves = [split(w) for w in inverses]
        crossed = [product(*w, *split(jnp.where(joined, tile, 0.0))) for w, tile in zip(halves, tiles)]
        inverses = [w - product(*split(c), *h) for w, c, h in zip(inverses, crossed, halves)]
        size *= 2
    return inverses


def solve_kernel(codes, counts, place, head_refs, side_refs, y_ref, out_ref, l_high, l_low, y_high, y_low, landing, head_sems, side_sems):
    rows, width = head_refs[0].shape[-2:]
    window = l_high.shape[0]
    per_row = len(head_refs) // len(codes)
    head_copies, side_copies = [], []
    for c, code in enumerate(codes):
        at = pl.ds(pl.multiple_of((place[0] ^ code) * rows, rows), rows)
        begin = c * sum(counts)
        for p in range(per_row):
            n = c * per_row + p
            into = landing.at[begin : begin + counts[p]]
            head_copies.append(pltpu.make_async_copy(head_refs[n], into, head_sems.at[n]))
            begin += counts[p]
        side_copies.append(pltpu.make_async_copy(side_refs[c], y_ref.at[at], side_sems.at[c]))
    for copy in head_copies + side_copies:
        copy.start()
    for c, code in enumerate(codes):
        at = pl.ds(pl.multiple_of((place[0] ^ code) * rows, rows), rows)
        n = c * sum(counts)
        for p in range(per_row):
            head_copies[c * per_row + p].wait()
            for k in range(counts[p]):
                across = pl.ds(pl.multiple_of(place[1 + n] * width, width), width)
                high, low = split(landing[n])
                l_high[at, across] = high
                l_low[at, across] = low
                n += 1
    for copy in side_copies:
        copy.wait()
    tiles = []
    for t in range(window // TILE):
        at = slice(t * TILE, (t + 1) * TILE)
        tiles.append(l_high[at, at].astype(F32) + l_low[at, at].astype(F32))
    inverses = half_inverses(tiles)
    ready = y_ref[:TILE]
    for t in range(window // TILE):
        begin = t * TILE
        value = ready
        if t:
            before = slice(begin - TILE, begin)
            at = slice(begin, begin + TILE)
            value = value - product(l_high[at, before], l_low[at, before], *solved)
        w = inverses[t]
        answers = []
        for h in range(TILE // HALF):
            part = value[h * HALF : (h + 1) * HALF]
            at = slice(begin + h * HALF, begin + (h + 1) * HALF)
            if h:
                inside = slice(begin, begin + h * HALF)
                part = part - product(l_high[at, inside], l_low[at, inside], *answers[0])
            inv = w[h * HALF : (h + 1) * HALF, h * HALF : (h + 1) * HALF]
            answer = product(*split(inv), *split(part))
            y_ref[at] = answer
            answers.append(split(answer))
            if h == 0 and begin + TILE < window:
                following = slice(begin + TILE, begin + 2 * TILE)
                ready = y_ref[following]
                if t:
                    ready = ready - product(
                        l_high[following, :begin], l_low[following, :begin], y_high[:begin], y_low[:begin]
                    )
        solved = [jnp.concatenate(both, axis=0) for both in zip(*answers)]
        y_high[begin : begin + TILE], y_low[begin : begin + TILE] = solved
    at = pl.ds(pl.multiple_of(place[0] * rows, rows), rows)
    copy = pltpu.make_async_copy(y_ref.at[at], out_ref.at[0, 0], side_sems.at[0])
    copy.start()
    copy.wait()


def solve(position, codes, heads, owners, sides, out_shape):
    counts = [part.shape[0] for part in heads[0]]
    window = sum(counts) * heads[0][0].shape[-1]
    columns = sides[0].shape[-1]
    flat = [part for parts in heads for part in parts]
    total = len(flat)
    place = jnp.concatenate([position] + [owners] * len(codes))

    def kernel(place, *refs):
        head_refs, side_refs = refs[:total], refs[total : total + len(codes)]
        solve_kernel(codes, counts, place, head_refs, side_refs, *refs[total + len(codes) :])

    return pl.pallas_call(
        kernel,
        out_shape=[jax.ShapeDtypeStruct((window, columns), F32), jax.ShapeDtypeStruct(out_shape, F32)],
        in_specs=[pl.BlockSpec(memory_space=pltpu.SMEM)] + [pl.BlockSpec(memory_space=pl.ANY)] * (total + len(codes)),
        out_specs=[pl.BlockSpec(memory_space=pltpu.VMEM), pl.BlockSpec(memory_space=pl.ANY)],
        scratch_shapes=[
            pltpu.VMEM((window, window), BF16),
            pltpu.VMEM((window, window), BF16),
            pltpu.VMEM((window, columns), BF16),
            pltpu.VMEM((window, columns), BF16),
            pltpu.VMEM((len(codes) * sum(counts), *flat[0].shape[1:]), F32),
            pltpu.SemaphoreType.DMA((total,)),
            pltpu.SemaphoreType.DMA((len(codes),)),
        ],
        compiler_params=pltpu.CompilerParams(vmem_limit_bytes=48 << 20),
        cost_estimate=pl.CostEstimate(
            flops=30 * window * window * columns, bytes_accessed=4 * window * (window + 2 * columns), transcendentals=0
        ),
        name="solve",
    )(place, *flat, *sides)


def load(places, begin, widths, y_ref, y_high, y_low):
    at = 0
    for n, width in enumerate(widths):
        high, low = split(y_ref[pl.ds(pl.multiple_of(places[begin + n] * width, width), width)])
        y_high[at : at + width] = high
        y_low[at : at + width] = low
        at += width


def update_first(y, places, pieces, base):
    flat = [part for piece in pieces for part in piece]
    blocks, rows, _ = flat[0].shape
    columns = y.shape[1]
    widths = [piece[0].shape[-1] for piece in pieces]
    count, depth = len(flat), sum(widths)
    step = next(n for n in (3, 2, 1) if blocks % n == 0)

    def kernel(place, y_ref, base_ref, *refs):
        piece_refs, (acc_ref, y_high, y_low, done) = refs[:count], refs[count:]
        load(place, 0, widths, y_ref, y_high, y_low)
        done[0] = 0

        def body(base_block, *piece_blocks):
            for n in range(step):
                parts = iter(piece_blocks)
                wide = [sum(next(parts)[n] for _ in piece) for piece in pieces]
                high, low = split(jnp.concatenate(wide, axis=1))
                value = base_block[n, 0] - product(high, low, y_high[...], y_low[...])
                acc_ref[done[0] + n] = value
            done[0] += step

        pltpu.emit_pipeline(
            body,
            grid=(blocks // step,),
            in_specs=[pl.BlockSpec((step, 1, rows, columns), lambda i: (i, 0, 0, 0))]
            + [pl.BlockSpec((step, rows, part.shape[-1]), lambda i: (i, 0, 0)) for part in flat],
        )(base_ref.at[pl.ds(1, blocks)], *piece_refs)

    anywhere = pl.BlockSpec(memory_space=pl.ANY)
    inside = pl.BlockSpec(memory_space=pltpu.VMEM)
    return pl.pallas_call(
        kernel,
        out_shape=pltpu.VMEM((blocks, rows, columns), F32),
        in_specs=[pl.BlockSpec(memory_space=pltpu.SMEM), inside] + [anywhere] * (1 + count),
        out_specs=inside,
        scratch_shapes=[
            pltpu.VMEM((depth, columns), BF16),
            pltpu.VMEM((depth, columns), BF16),
            pltpu.SMEM((1,), jnp.int32),
        ],
        compiler_params=pltpu.CompilerParams(vmem_limit_bytes=44 << 20),
        cost_estimate=pl.CostEstimate(
            flops=6 * blocks * rows * depth * columns,
            bytes_accessed=4 * blocks * rows * (depth + 2 * columns),
            transcendentals=0,
        ),
        name="update_first",
    )(places, y, base, *flat)


def update_last(y, places, pieces, acc, target):
    flat = [part for piece in pieces for laid in piece for part in laid]
    blocks, rows, columns = acc.shape
    widths = [piece[0][0].shape[-1] for piece in pieces]
    count, depth = len(flat), sum(widths)

    def kernel(place, y_ref, acc_ref, *refs):
        piece_refs = refs[:count]
        out_ref, y_high, y_low, done, sems = refs[count + 1 :]
        load(place, 0, widths, y_ref, y_high, y_low)
        copies = []
        for i in range(blocks):
            at, wide = 0, []
            for piece in pieces:
                value = 0
                for laid in piece:
                    begin = 0
                    for part in laid:
                        if begin <= i < begin + part.shape[0]:
                            value = value + piece_refs[at][i - begin]
                        begin += part.shape[0]
                        at += 1
                wide.append(value)
            high, low = split(jnp.concatenate(wide, axis=1))
            done[i] = acc_ref[i] - product(high, low, y_high[...], y_low[...])
            copies.append(pltpu.make_async_copy(done.at[i], out_ref.at[i + 1, 0], sems.at[i]))
            copies[-1].start()
        for copy in copies:
            copy.wait()

    anywhere = pl.BlockSpec(memory_space=pl.ANY)
    inside = pl.BlockSpec(memory_space=pltpu.VMEM)
    return pl.pallas_call(
        kernel,
        out_shape=jax.ShapeDtypeStruct(target.shape, F32),
        in_specs=[pl.BlockSpec(memory_space=pltpu.SMEM)] + [inside] * (2 + count) + [anywhere],
        out_specs=anywhere,
        scratch_shapes=[
            pltpu.VMEM((depth, columns), BF16),
            pltpu.VMEM((depth, columns), BF16),
            pltpu.VMEM((blocks, rows, columns), F32),
            pltpu.SemaphoreType.DMA((blocks,)),
        ],
        input_output_aliases={3 + count: 0},
        compiler_params=pltpu.CompilerParams(vmem_limit_bytes=44 << 20),
        cost_estimate=pl.CostEstimate(
            flops=6 * blocks * rows * depth * columns,
            bytes_accessed=4 * blocks * rows * (depth + 2 * columns),
            transcendentals=0,
        ),
        name="update_last",
    )(places, y, pltpu.with_memory_space_constraint(acc, pltpu.VMEM), *flat, target)


def over_row(block, size):
    codes, held = [0], [block]
    bit = size // 2
    while bit:
        pairs = [(n, n ^ bit) for n in range(size)]
        held = held + [lax.ppermute(value, "row", pairs) for value in held]
        codes = codes + [code ^ bit for code in codes]
        bit //= 2
    return codes, held


def after(value, *others):
    return lax.optimization_barrier((value, *others))[0]


def body(right_sides, factor):
    row_count, real_count = lax.axis_size("row"), lax.axis_size("real")
    position = lax.axis_index("row")[None]
    mine = factor[:, 0]
    if real_count != 8:
        codes, sides = over_row(right_sides[0, 0], row_count)
        head = lax.all_gather(mine[0], "real", axis=1, tiled=True)
        codes, heads = over_row(head[None], row_count)
        whole = jnp.zeros((1,), jnp.int32)
        y, result = solve(position, codes, [[part] for part in heads], whole, sides, right_sides.shape)
        rest = lax.all_gather(mine[1:], "real", axis=2, tiled=True)
        half = rest.shape[2] // 2
        acc = update_first(y, whole, [[rest[:, :, :half]]], right_sides)
        return update_last(y, whole + 1, [[[rest[:, :, half:]]]], acc, result)

    lanes = 2
    here = lax.axis_index("real")
    z, side = here // lanes, here % lanes
    outer = (z == 0) | (z == 3)
    pick = lambda a, b: jnp.where(outer, a, b)
    mirror = 3 - z
    partner = z ^ 1
    other = mirror ^ 1
    spot = lambda at, which: at * lanes + which

    def hop(value, bits):
        return lax.ppermute(value, "real", [(n, n ^ bits) for n in range(real_count)])

    def move(value, pairs):
        return lax.ppermute(value, "real", [(a * lanes + n, b * lanes + n) for a, b in pairs for n in range(lanes)])

    ends = lambda value: hop(value, 2)
    lane = lambda value: hop(value, 1)
    middle = lambda value: move(value, [(1, 2), (2, 1)])
    out = lambda value: move(value, [(1, 0), (2, 3)])

    trailing = mine.shape[0] - 1
    cut = (trailing + 1) // 2
    own = mine[1:]
    halves = [slice(0, cut), slice(cut, trailing)]

    h_own = mine[0:1]
    h_line = [h_own] + [hop(h_own, bits) for bits in (2, 4, 6)]
    middle_row = trailing // 2
    s1 = [lane(own[:middle_row]), None]
    start = after(own, h_line[1])
    e1, m1 = ends(start), middle(start)
    far_head = h_line[2]
    h_line = jnp.concatenate(h_line)
    h_all = jnp.concatenate([h_line, lane(h_line)])
    s1[1] = lane(after(own[middle_row:], s1[0]))
    s1 = jnp.concatenate(s1)
    owners = jnp.stack([here ^ bits for bits in (0, 2, 4, 6, 1, 3, 5, 7)]).astype(jnp.int32)
    codes, sides = over_row(after(right_sides, far_head)[0, 0], row_count)
    codes, heads = over_row(after(h_all, sides[1]), row_count)

    first, second = halves
    o2 = out(after(m1, e1))
    m2 = middle(e1)
    s2 = lane(after(e1, s1))
    o3 = [out(m2[rows]) for rows in halves]
    both = [pick(o2, m2)[rows] for rows in halves]
    s3 = [lane(after(both[0], s2)), None]
    heads[0] = after(heads[0], o2, m2)
    y, result = solve(position, codes, [[part] for part in heads], owners, sides, right_sides.shape)
    s3[1] = lane(after(both[1], y))
    last = [ends(after(s3[0], y, o3[1])), lane(pick(o3[1], m1[second]))]

    near_y = [
        here,
        spot(partner, side),
        spot(z, 1 - side),
        pick(spot(other, side), spot(mirror, side)),
        spot(partner, 1 - side),
    ]
    far_y = [pick(spot(mirror, side), spot(other, side)), spot(other, 1 - side), spot(mirror, 1 - side)]
    near_y, far_y = (jnp.stack(places).astype(jnp.int32) for places in (near_y, far_y))
    inside = lambda parts: [pltpu.with_memory_space_constraint(part, pltpu.VMEM) for part in parts]
    acc = update_first(y, near_y, [[own], [e1], [s1], [m1, o2], [s2]], right_sides)
    return update_last(y, far_y, [[[m2], o3], [s3], [inside(last)]], acc, result)


def solution(mesh):
    placed = (P(None, "row", None, "real"), P(None, "row", None, "real"))
    return jax.shard_map(
        body, mesh=mesh, in_specs=placed, out_specs=P(None, "row", None, "real"), check_vma=False
    )
```

```python
import functools
import math

import jax
import jax.numpy as jnp
from jax import lax
from jax.experimental import pallas as pl
from jax.experimental.pallas import tpu as pltpu
from jax.sharding import PartitionSpec as P

F32, BF16 = jnp.float32, jnp.bfloat16
TILE, HALF, BASE = 128, 64, 16


def split(value):
    high = value.astype(BF16)
    return high, (value - high.astype(F32)).astype(BF16)


def product(a_high, a_low, b_high, b_low):
    wide = jnp.concatenate([a_high, a_low, a_high], axis=1)
    tall = jnp.concatenate([b_high, b_high, b_low], axis=0)
    return jnp.dot(wide, tall, preferred_element_type=F32)


def half_inverses(tiles):
    count = len(tiles)
    lane = lax.broadcasted_iota(jnp.int32, (BASE, TILE), 1)
    row = lax.broadcasted_iota(jnp.int32, (BASE, TILE), 0)
    packed = []
    for tile in tiles:
        kept = jnp.zeros((BASE, TILE), F32)
        for g in range(TILE // BASE):
            kept = jnp.where(lane // BASE == g, tile[g * BASE : (g + 1) * BASE], kept)
        packed.append(kept)
    packed = jnp.concatenate(packed, axis=0)
    k = lax.broadcasted_iota(jnp.int32, (TILE, TILE), 0)
    m = lax.broadcasted_iota(jnp.int32, (TILE, TILE), 1)
    high, rest = split(packed)
    middle = (packed - high.astype(F32) - rest.astype(F32)).astype(BF16)
    parts = jnp.concatenate([high, rest, middle], axis=1)
    columns = []
    for j in range(BASE):
        spread = (k == (m // BASE) * BASE + j).astype(F32).astype(BF16)
        tall = jnp.concatenate([spread] * 3, axis=0)
        columns.append(jnp.dot(parts, tall, preferred_element_type=F32).reshape(count, BASE, TILE))
    diagonal = columns[0]
    for j in range(1, BASE):
        diagonal = jnp.where(row[None] == j, columns[j], diagonal)
    scale = 1.0 / diagonal
    x = jnp.where((row == lane % BASE)[None], scale, 0.0)
    for j in range(BASE - 1):
        x = x - jnp.where(row[None] > j, columns[j] * scale, 0.0) * x[:, j : j + 1]
    inverses = [
        jnp.where(k // BASE == m // BASE, jnp.concatenate([x[t]] * (TILE // BASE), axis=0), 0.0) for t in range(count)
    ]
    size = BASE
    while size < HALF:
        joined = (k // (2 * size) == m // (2 * size)) & (k // size != m // size)
        halves = [split(w) for w in inverses]
        crossed = [product(*w, *split(jnp.where(joined, tile, 0.0))) for w, tile in zip(halves, tiles)]
        inverses = [w - product(*split(c), *h) for w, c, h in zip(inverses, crossed, halves)]
        size *= 2
    return inverses


def solve_kernel(codes, counts, place, head_refs, side_refs, y_ref, out_ref, l_high, l_low, y_high, y_low, landing, head_sems, side_sems):
    rows, width = head_refs[0].shape[-2:]
    window = l_high.shape[0]
    per_row = len(head_refs) // len(codes)
    head_copies, side_copies = [], []
    for c, code in enumerate(codes):
        at = pl.ds(pl.multiple_of((place[0] ^ code) * rows, rows), rows)
        begin = c * sum(counts)
        for p in range(per_row):
            n = c * per_row + p
            into = landing.at[begin : begin + counts[p]]
            head_copies.append(pltpu.make_async_copy(head_refs[n], into, head_sems.at[n]))
            begin += counts[p]
        side_copies.append(pltpu.make_async_copy(side_refs[c], y_ref.at[at], side_sems.at[c]))
    for copy in head_copies + side_copies:
        copy.start()
    for c, code in enumerate(codes):
        at = pl.ds(pl.multiple_of((place[0] ^ code) * rows, rows), rows)
        n = c * sum(counts)
        for p in range(per_row):
            head_copies[c * per_row + p].wait()
            for k in range(counts[p]):
                across = pl.ds(pl.multiple_of(place[1 + n] * width, width), width)
                high, low = split(landing[n])
                l_high[at, across] = high
                l_low[at, across] = low
                n += 1
    for copy in side_copies:
        copy.wait()
    tiles = []
    for t in range(window // TILE):
        at = slice(t * TILE, (t + 1) * TILE)
        tiles.append(l_high[at, at].astype(F32) + l_low[at, at].astype(F32))
    inverses = half_inverses(tiles)
    ready = y_ref[:TILE]
    for t in range(window // TILE):
        begin = t * TILE
        value = ready
        if t:
            before = slice(begin - TILE, begin)
            at = slice(begin, begin + TILE)
            value = value - product(l_high[at, before], l_low[at, before], *solved)
        w = inverses[t]
        answers = []
        for h in range(TILE // HALF):
            part = value[h * HALF : (h + 1) * HALF]
            at = slice(begin + h * HALF, begin + (h + 1) * HALF)
            if h:
                inside = slice(begin, begin + h * HALF)
                part = part - product(l_high[at, inside], l_low[at, inside], *answers[0])
            inv = w[h * HALF : (h + 1) * HALF, h * HALF : (h + 1) * HALF]
            answer = product(*split(inv), *split(part))
            y_ref[at] = answer
            answers.append(split(answer))
            if h == 0 and begin + TILE < window:
                following = slice(begin + TILE, begin + 2 * TILE)
                ready = y_ref[following]
                if t:
                    ready = ready - product(
                        l_high[following, :begin], l_low[following, :begin], y_high[:begin], y_low[:begin]
                    )
        solved = [jnp.concatenate(both, axis=0) for both in zip(*answers)]
        y_high[begin : begin + TILE], y_low[begin : begin + TILE] = solved
    at = pl.ds(pl.multiple_of(place[0] * rows, rows), rows)
    copy = pltpu.make_async_copy(y_ref.at[at], out_ref.at[0, 0], side_sems.at[0])
    copy.start()
    copy.wait()


def solve(position, codes, heads, owners, sides, out_shape):
    counts = [part.shape[0] for part in heads[0]]
    window = sum(counts) * heads[0][0].shape[-1]
    columns = sides[0].shape[-1]
    flat = [part for parts in heads for part in parts]
    total = len(flat)
    place = jnp.concatenate([position] + [owners] * len(codes))

    def kernel(place, *refs):
        head_refs, side_refs = refs[:total], refs[total : total + len(codes)]
        solve_kernel(codes, counts, place, head_refs, side_refs, *refs[total + len(codes) :])

    return pl.pallas_call(
        kernel,
        out_shape=[jax.ShapeDtypeStruct((window, columns), F32), jax.ShapeDtypeStruct(out_shape, F32)],
        in_specs=[pl.BlockSpec(memory_space=pltpu.SMEM)] + [pl.BlockSpec(memory_space=pl.ANY)] * (total + len(codes)),
        out_specs=[pl.BlockSpec(memory_space=pltpu.VMEM), pl.BlockSpec(memory_space=pl.ANY)],
        scratch_shapes=[
            pltpu.VMEM((window, window), BF16),
            pltpu.VMEM((window, window), BF16),
            pltpu.VMEM((window, columns), BF16),
            pltpu.VMEM((window, columns), BF16),
            pltpu.VMEM((len(codes) * sum(counts), *flat[0].shape[1:]), F32),
            pltpu.SemaphoreType.DMA((total,)),
            pltpu.SemaphoreType.DMA((len(codes),)),
        ],
        compiler_params=pltpu.CompilerParams(vmem_limit_bytes=48 << 20),
        cost_estimate=pl.CostEstimate(
            flops=30 * window * window * columns, bytes_accessed=4 * window * (window + 2 * columns), transcendentals=0
        ),
        name="solve",
    )(place, *flat, *sides)


def load(places, begin, widths, y_ref, y_high, y_low):
    at = 0
    for n, width in enumerate(widths):
        high, low = split(y_ref[pl.ds(pl.multiple_of(places[begin + n] * width, width), width)])
        y_high[at : at + width] = high
        y_low[at : at + width] = low
        at += width


def update_first(y, places, pieces, base):
    flat = [part for piece in pieces for part in piece]
    blocks, rows, _ = flat[0].shape
    columns = y.shape[1]
    widths = [piece[0].shape[-1] for piece in pieces]
    count, depth = len(flat), sum(widths)
    step = next(n for n in (3, 2, 1) if blocks % n == 0)

    def kernel(place, y_ref, base_ref, *refs):
        piece_refs, (acc_ref, y_high, y_low, done) = refs[:count], refs[count:]
        load(place, 0, widths, y_ref, y_high, y_low)
        done[0] = 0

        def body(base_block, *piece_blocks):
            for n in range(step):
                parts = iter(piece_blocks)
                wide = [sum(next(parts)[n] for _ in piece) for piece in pieces]
                high, low = split(jnp.concatenate(wide, axis=1))
                value = base_block[n, 0] - product(high, low, y_high[...], y_low[...])
                acc_ref[done[0] + n] = value
            done[0] += step

        pltpu.emit_pipeline(
            body,
            grid=(blocks // step,),
            in_specs=[pl.BlockSpec((step, 1, rows, columns), lambda i: (i, 0, 0, 0))]
            + [pl.BlockSpec((step, rows, part.shape[-1]), lambda i: (i, 0, 0)) for part in flat],
        )(base_ref.at[pl.ds(1, blocks)], *piece_refs)

    anywhere = pl.BlockSpec(memory_space=pl.ANY)
    inside = pl.BlockSpec(memory_space=pltpu.VMEM)
    return pl.pallas_call(
        kernel,
        out_shape=pltpu.VMEM((blocks, rows, columns), F32),
        in_specs=[pl.BlockSpec(memory_space=pltpu.SMEM), inside] + [anywhere] * (1 + count),
        out_specs=inside,
        scratch_shapes=[
            pltpu.VMEM((depth, columns), BF16),
            pltpu.VMEM((depth, columns), BF16),
            pltpu.SMEM((1,), jnp.int32),
        ],
        compiler_params=pltpu.CompilerParams(vmem_limit_bytes=44 << 20),
        cost_estimate=pl.CostEstimate(
            flops=6 * blocks * rows * depth * columns,
            bytes_accessed=4 * blocks * rows * (depth + 2 * columns),
            transcendentals=0,
        ),
        name="update_first",
    )(places, y, base, *flat)


def update_last(y, places, pieces, acc, target):
    flat = [part for piece in pieces for laid in piece for part in laid]
    blocks, rows, columns = acc.shape
    widths = [piece[0][0].shape[-1] for piece in pieces]
    count, depth = len(flat), sum(widths)

    def kernel(place, y_ref, acc_ref, *refs):
        piece_refs = refs[:count]
        out_ref, y_high, y_low, done, sems = refs[count + 1 :]
        load(place, 0, widths, y_ref, y_high, y_low)
        copies = []
        for i in range(blocks):
            at, wide = 0, []
            for piece in pieces:
                value = 0
                for laid in piece:
                    begin = 0
                    for part in laid:
                        if begin <= i < begin + part.shape[0]:
                            value = value + piece_refs[at][i - begin]
                        begin += part.shape[0]
                        at += 1
                wide.append(value)
            high, low = split(jnp.concatenate(wide, axis=1))
            done[i] = acc_ref[i] - product(high, low, y_high[...], y_low[...])
            copies.append(pltpu.make_async_copy(done.at[i], out_ref.at[i + 1, 0], sems.at[i]))
            copies[-1].start()
        for copy in copies:
            copy.wait()

    anywhere = pl.BlockSpec(memory_space=pl.ANY)
    inside = pl.BlockSpec(memory_space=pltpu.VMEM)
    return pl.pallas_call(
        kernel,
        out_shape=jax.ShapeDtypeStruct(target.shape, F32),
        in_specs=[pl.BlockSpec(memory_space=pltpu.SMEM)] + [inside] * (2 + count) + [anywhere],
        out_specs=anywhere,
        scratch_shapes=[
            pltpu.VMEM((depth, columns), BF16),
            pltpu.VMEM((depth, columns), BF16),
            pltpu.VMEM((blocks, rows, columns), F32),
            pltpu.SemaphoreType.DMA((blocks,)),
        ],
        input_output_aliases={3 + count: 0},
        compiler_params=pltpu.CompilerParams(vmem_limit_bytes=44 << 20),
        cost_estimate=pl.CostEstimate(
            flops=6 * blocks * rows * depth * columns,
            bytes_accessed=4 * blocks * rows * (depth + 2 * columns),
            transcendentals=0,
        ),
        name="update_last",
    )(places, y, pltpu.with_memory_space_constraint(acc, pltpu.VMEM), *flat, target)


def over_row(block, size):
    codes, held = [0], [block]
    bit = size // 2
    while bit:
        pairs = [(n, n ^ bit) for n in range(size)]
        held = held + [lax.ppermute(value, "row", pairs) for value in held]
        codes = codes + [code ^ bit for code in codes]
        bit //= 2
    return codes, held


def after(value, *others):
    return lax.optimization_barrier((value, *others))[0]


def body(right_sides, factor):
    row_count, real_count = lax.axis_size("row"), lax.axis_size("real")
    position = lax.axis_index("row")[None]
    mine = factor[:, 0]
    if real_count != 8:
        codes, sides = over_row(right_sides[0, 0], row_count)
        head = lax.all_gather(mine[0], "real", axis=1, tiled=True)
        codes, heads = over_row(head[None], row_count)
        whole = jnp.zeros((1,), jnp.int32)
        y, result = solve(position, codes, [[part] for part in heads], whole, sides, right_sides.shape)
        rest = lax.all_gather(mine[1:], "real", axis=2, tiled=True)
        half = rest.shape[2] // 2
        acc = update_first(y, whole, [[rest[:, :, :half]]], right_sides)
        return update_last(y, whole + 1, [[[rest[:, :, half:]]]], acc, result)

    lanes = 2
    here = lax.axis_index("real")
    z, side = here // lanes, here % lanes
    outer = (z == 0) | (z == 3)
    pick = lambda a, b: jnp.where(outer, a, b)
    mirror = 3 - z
    partner = z ^ 1
    other = mirror ^ 1
    spot = lambda at, which: at * lanes + which

    def hop(value, bits):
        return lax.ppermute(value, "real", [(n, n ^ bits) for n in range(real_count)])

    def move(value, pairs):
        return lax.ppermute(value, "real", [(a * lanes + n, b * lanes + n) for a, b in pairs for n in range(lanes)])

    ends = lambda value: hop(value, 2)
    lane = lambda value: hop(value, 1)
    middle = lambda value: move(value, [(1, 2), (2, 1)])
    out = lambda value: move(value, [(1, 0), (2, 3)])

    trailing = mine.shape[0] - 1
    cut = (trailing + 1) // 2
    own = mine[1:]
    halves = [slice(0, cut), slice(cut, trailing)]

    h_own = mine[0:1]
    h_line = [h_own] + [hop(h_own, bits) for bits in (2, 4, 6)]
    middle_row = trailing // 2
    s1 = [lane(own[:middle_row]), None]
    start = after(own, h_line[1])
    e1, m1 = ends(start), middle(start)
    far_head = h_line[2]
    h_line = jnp.concatenate(h_line)
    h_all = jnp.concatenate([h_line, lane(h_line)])
    s1[1] = lane(after(own[middle_row:], s1[0]))
    s1 = jnp.concatenate(s1)
    owners = jnp.stack([here ^ bits for bits in (0, 2, 4, 6, 1, 3, 5, 7)]).astype(jnp.int32)
    codes, sides = over_row(after(right_sides, far_head)[0, 0], row_count)
    codes, heads = over_row(after(h_all, sides[1]), row_count)

    first, second = halves
    o2 = out(m1)
    m2 = middle(e1)
    s2 = lane(after(e1, s1))
    o3 = [out(m2[rows]) for rows in halves]
    both = [pick(o2, m2)[rows] for rows in halves]
    s3 = [lane(after(both[0], s2)), None]
    heads[0] = after(heads[0], o2, m2)
    y, result = solve(position, codes, [[part] for part in heads], owners, sides, right_sides.shape)
    s3[1] = lane(after(both[1], y))
    last = [ends(after(s3[0], y, o3[1])), lane(pick(o3[1], m1[second]))]

    near_y = [
        here,
        spot(partner, side),
        spot(z, 1 - side),
        pick(spot(other, side), spot(mirror, side)),
        spot(partner, 1 - side),
    ]
    far_y = [pick(spot(mirror, side), spot(other, side)), spot(other, 1 - side), spot(mirror, 1 - side)]
    near_y, far_y = (jnp.stack(places).astype(jnp.int32) for places in (near_y, far_y))
    inside = lambda parts: [pltpu.with_memory_space_constraint(part, pltpu.VMEM) for part in parts]
    acc = update_first(y, near_y, [[own], [e1], [s1], [m1, o2], [s2]], right_sides)
    return update_last(y, far_y, [[[m2], o3], [s3], [inside(last)]], acc, result)


def solution(mesh):
    placed = (P(None, "row", None, "real"), P(None, "row", None, "real"))
    return jax.shard_map(
        body, mesh=mesh, in_specs=placed, out_specs=P(None, "row", None, "real"), check_vma=False
    )
```
